32 devices in a mesh: ctx: 8 (over z, y), head: 4 (over x, core).
Axes of the slice: x: 2, y: 2, z: 4, core: 2. Of those that a mesh axis runs over, the one named last changes fastest.
Arguments:
- queries: bfloat16 [4032, 4096], P('ctx', 'head'), may hold values from -6 to 6
- keys: bfloat16 [4032, 4096], P('ctx', 'head'), may hold values from -6 to 6
- values: bfloat16 [4032, 4096], P('ctx', 'head'), may hold values from -6 to 6
- out_weight: bfloat16 [4096, 4096], P('head'), may hold values from -0.09375 to 0.09375
- norm_gain: float32 [4096], P('head'), may hold values from 0.1 to 1.9
- tile_counts: int32 [8], replicated, may hold values from 1 to 63, as said below
- route_device: int32 [504], P('ctx'), may hold values from -1 to 7, as said below
- route_slot: int32 [504], P('ctx'), may hold values from -1 to 31, as said below
- session_starts: int32 [4], replicated, may hold values from 0 to 2047, as said below
Outputs:
- balanced_out: bfloat16 [2048, 4096], P('ctx', 'head')
The draws below stay inside these ranges and needn't reach their ends.
Inputs may be any that keep to these rules, and one draw needn't show every extreme that they name: `tile_counts`: each value is at least 1 and the values sum to 256; some index has exactly 63 live tiles. `route_device`: the live tiles of an index are its first tile_counts slots; dead slots hold -1; each index of ctx receives exactly 32 tiles, and no index sends more than 8 tiles to one index. `route_slot`: dead slots hold -1; every pair of receiving index and slot below 32 is named by exactly one live tile. `session_starts`: strictly increasing, first value 0, last value 2048 - 1.
All inputs are finite; a program needn't handle non-finite values.
Results may differ from the reference program's by a relative error of at most 0.018.
Values may be sent and summed in bfloat16 or wider, within the bound.
A program may use at most 128 MiB of HBM per device.

```python
import jax
import jax.numpy as jnp
from jax import lax

D = 4096
HEADS = 32
DH = 128
CH = 8
BAL = 32
SESSIONS = 4
SLOTS = 63
ROWS = 4032
LIVE = 2048
N_CTX = 8
N_HEAD = 4


def counts_helper(key):
    ordering = jax.random.permutation(jax.random.fold_in(key, 11), N_CTX)
    spread = jax.random.randint(jax.random.fold_in(key, 12), (N_CTX // 2,), 0, BAL)
    spread = spread.at[0].set(BAL - 1)
    counts = jnp.zeros((N_CTX,), jnp.int32)
    counts = counts.at[ordering[0::2]].set(BAL + spread)
    counts = counts.at[ordering[1::2]].set(BAL - spread)
    return counts.astype(jnp.int32)


def route_helper(key):
    counts = counts_helper(key)
    first = jnp.cumsum(counts) - counts
    column = jnp.arange(SLOTS, dtype=jnp.int32)[None, :]
    global_index = first[:, None] + column
    is_live = column < counts[:, None]
    shuffle = jax.random.permutation(jax.random.fold_in(key, 13), N_CTX).astype(jnp.int32)
    device = jnp.where(is_live, shuffle[global_index % N_CTX], -1)
    row_keys = jax.random.split(jax.random.fold_in(key, 15), N_CTX)
    slot_orders = jax.vmap(lambda one_key: jax.random.permutation(one_key, BAL))(row_keys).astype(jnp.int32)
    safe_device = jnp.maximum(device, 0)
    safe_rank = jnp.minimum(global_index // N_CTX, BAL - 1)
    target = jnp.where(is_live, slot_orders[safe_device, safe_rank], -1)
    return (device.reshape(-1).astype(jnp.int32), target.reshape(-1).astype(jnp.int32))


def draw_tile_counts(key, part):
    return counts_helper(key)


def draw_route_device(key, part):
    return route_helper(key)[0]


def draw_route_slot(key, part):
    return route_helper(key)[1]


def draw_session_starts(key, part):
    picks = jax.random.permutation(jax.random.fold_in(key, 14), LIVE - 2)[:SESSIONS - 2] + 1
    middle = jnp.sort(picks).astype(jnp.int32)
    return jnp.concatenate([jnp.zeros((1,), jnp.int32), middle, jnp.full((1,), LIVE - 1, jnp.int32)]).astype(jnp.int32)


def shard_levels(own_key, shape, pieces, smallest, high):
    def one(position, shards_of):
        heights = jax.random.uniform(jax.random.fold_in(jax.random.fold_in(own_key, 6), position), (shards_of,), jnp.float32, smallest / len(pieces), high / len(pieces))
        return jnp.repeat(jnp.exp(heights), shape[position] // shards_of).reshape((-1,) + (1,) * (len(shape) - position - 1))

    level = one(*pieces[0])
    for cut in pieces[1:]:
        level = level * one(*cut)
    return level


def bell_draw(stream_key, shape, scale, bound, shards=(), held_as=jnp.bfloat16):
    loudness = shard_levels(stream_key, shape, shards, -0.22, 0.18) if shards else 1.0
    entries = jax.random.normal(stream_key, shape, jnp.float32) * scale * loudness
    return jnp.minimum(jnp.maximum(entries, -bound), bound).astype(held_as)


def setup_inputs(seed: int = 0) -> dict:
    arg_keys = jax.random.split(jax.random.key(seed), 10)
    queries = bell_draw(arg_keys[0], (ROWS, D), 1.0, 6.0, ((0, 8), (1, 4)))
    keys = bell_draw(arg_keys[1], (ROWS, D), 1.0, 6.0, ((0, 8), (1, 4)))
    values = bell_draw(arg_keys[2], (ROWS, D), 1.0, 6.0, ((0, 8), (1, 4)))
    out_weight = bell_draw(arg_keys[3], (D, D), D ** -0.5, 0.09375, ((0, 4),))
    norm_gain = jnp.clip(1.0 + 0.18 * jax.random.normal(arg_keys[4], (D,), jnp.float32), 0.1, 1.9)
    tile_counts = draw_tile_counts(jax.random.fold_in(arg_keys[9], 71), 0)
    route_device = draw_route_device(jax.random.fold_in(arg_keys[9], 71), 0)
    route_slot = draw_route_slot(jax.random.fold_in(arg_keys[9], 71), 0)
    session_starts = draw_session_starts(jax.random.fold_in(arg_keys[9], 71), 0)
    return {"queries": queries, "keys": keys, "values": values, "out_weight": out_weight, "norm_gain": norm_gain, "tile_counts": tile_counts, "route_device": route_device, "route_slot": route_slot, "session_starts": session_starts}


EPSILON = 1e-06

def feature(block):
    value = block.astype(jnp.float32)
    return jnp.where(value > 0, value + 1.0, jnp.exp(jnp.minimum(value, 0.0))).astype(jnp.bfloat16)

def reference(queries, keys, values, out_weight, norm_gain, tile_counts, route_device, route_slot, session_starts):
    tile_total = N_CTX * SLOTS
    query_feature_map = feature(queries).reshape(tile_total, CH, HEADS, DH)
    key_map = feature(keys).reshape(tile_total, CH, HEADS, DH)
    value_row_block = values.reshape(tile_total, CH, HEADS, DH)
    first_tile = (jnp.cumsum(tile_counts) - tile_counts).astype(jnp.int32)
    tile_ids = jnp.arange(tile_total, dtype=jnp.int32)
    tile_dev = tile_ids // SLOTS
    tile_col = tile_ids % SLOTS
    tile_live = tile_col < tile_counts[tile_dev]
    positions = (CH * (first_tile[tile_dev] + tile_col))[:, None] + jnp.arange(CH, dtype=jnp.int32)[None, :]
    sessions = (lax.optimization_barrier(jnp.sum((session_starts[None, None, :] <= positions[:, :, None]).astype(jnp.int32), axis=2)) - 1).astype(jnp.int32)
    causal = jnp.arange(CH)[None, :] <= jnp.arange(CH)[:, None]

    def advance(carried, inputs):
        key_value_state, carry_sess = carried
        q_tile, k_tile, v_tile, s_tile, l_tile = inputs
        query_float = q_tile.astype(jnp.float32)
        k_float = k_tile.astype(jnp.float32)
        value_float = v_tile.astype(jnp.float32)
        allowed = causal & (s_tile[None, :] == s_tile[:, None])
        scores = jnp.einsum('thd,shd->hts', query_float, k_float, precision=lax.Precision.HIGHEST)
        scores = jnp.where(allowed[None], scores, 0.0)
        inside = jnp.einsum('hts,shd->thd', scores, value_float, precision=lax.Precision.HIGHEST)
        carried_portion = jnp.einsum('ycu,cux->ycx', query_float, key_value_state, precision=lax.Precision.HIGHEST)
        carried_portion = jnp.where((s_tile == carry_sess)[:, None, None], carried_portion, 0.0)
        numerator = inside + carried_portion
        last_sess = s_tile[CH - 1]
        selected_rows = jnp.where((s_tile == last_sess)[:, None, None], k_float, 0.0)
        appended_term = jnp.einsum('pld,plw->ldw', selected_rows, value_float, precision=lax.Precision.HIGHEST)
        new_state = jnp.where(carry_sess == last_sess, key_value_state, 0.0) + appended_term
        key_value_state = jnp.where(l_tile, new_state, key_value_state)
        carry_sess = jnp.where(l_tile, last_sess, carry_sess).astype(jnp.int32)
        return ((key_value_state, carry_sess), numerator)
    initial = (jnp.zeros((HEADS, DH, DH), jnp.float32), jnp.array(-1, jnp.int32))
    _, numerators = lax.scan(advance, initial, (query_feature_map, key_map, value_row_block, sessions, tile_live))
    inverse_rms = lax.rsqrt(lax.optimization_barrier(jnp.mean(numerators * numerators, axis=-1, keepdims=True)) + EPSILON)
    attended = (numerators * inverse_rms * norm_gain.reshape(HEADS, DH)).astype(jnp.bfloat16).reshape(tile_total, CH, D)
    destination = jnp.where(route_device >= 0, route_device * BAL + route_slot, N_CTX * BAL).astype(jnp.int32)
    balanced = jnp.zeros((N_CTX * BAL, CH, D), jnp.bfloat16).at[destination].set(attended, mode='drop')
    balanced = balanced.reshape(N_CTX * BAL * CH, D)
    group_width = D // N_HEAD
    summed = jnp.zeros((N_CTX * BAL * CH, D), jnp.float32)
    for group_index in range(N_HEAD):
        lower = group_index * group_width
        partial_value = jnp.dot(balanced[:, lower:lower + group_width].astype(jnp.float32), out_weight[lower:lower + group_width].astype(jnp.float32), precision=lax.Precision.HIGHEST)
        summed = summed + partial_value.astype(jnp.bfloat16).astype(jnp.float32)
    return summed.astype(jnp.bfloat16)
```

```python
import jax
import jax.numpy as jnp
from jax import lax
from jax.sharding import PartitionSpec as P

DH = 128
CH = 8
BAL = 32


EPSILON = 1e-06


def carried_in(x, axis, combine, identity):
    count, here = (lax.axis_size(axis), lax.axis_index(axis))
    everything = jax.tree.map(
        lambda part, kind: lax.all_gather(part.astype(kind), axis), x, (jnp.bfloat16, jnp.bfloat16)
    )
    start = jax.tree.map(
        lambda part, zero: jnp.broadcast_to(jnp.asarray(zero, part.dtype), part.shape), x, identity
    )

    def step(k, before):
        reached = k < here
        new = combine(
            before, jax.tree.map(lambda part, own: part[k].astype(own.dtype), everything, x)
        )
        return jax.tree.map(lambda a, b: jnp.where(reached, a, b), new, before)

    return lax.fori_loop(0, count, step, start)


def feature(block):
    value = block.astype(jnp.float32)
    return jnp.where(value > 0, value + 1.0, jnp.exp(jnp.minimum(value, 0.0))).astype(jnp.bfloat16)


def split_parts(matrix):
    upper = matrix.astype(jnp.bfloat16)
    lower = (matrix - upper.astype(jnp.float32)).astype(jnp.bfloat16)
    return (upper, lower)


def session_of(session_starts, position):
    return jnp.sum((session_starts[None, :] <= position[:, None]).astype(jnp.int32), axis=1) - 1


def combine_states(earlier, later):
    return (jnp.maximum(earlier[0], later[0]), later[1] + (1.0 - later[0]) * earlier[1])


def deliver(payload, route_device, route_slot, ctx_size):
    slot_count = route_device.shape[0]
    columns = payload.shape[1]
    capacity = (slot_count + ctx_size - 1) // ctx_size
    tile_rows = payload.reshape(slot_count, CH * columns)
    ordinal = jnp.arange(slot_count)
    clashes = (route_device[None, :] == route_device[:, None]) & (
        ordinal[None, :] < ordinal[:, None]
    )
    before = jnp.sum(clashes.astype(jnp.int32), axis=1)
    target = jnp.where(route_device >= 0, route_device * capacity + before, -1)
    buckets = jnp.arange(ctx_size * capacity)
    chosen = buckets[:, None] == target[None, :]
    outgoing = jnp.dot(
        chosen.astype(jnp.bfloat16), tile_rows, preferred_element_type=jnp.float32
    ).astype(jnp.bfloat16)
    labels = jnp.sum(jnp.where(chosen, route_slot[None, :] + 1, 0), axis=1) - 1
    arrived, arrived_labels = (
        lax.all_to_all(outgoing, "ctx", split_axis=0, concat_axis=0, tiled=True),
        lax.all_to_all(labels, "ctx", split_axis=0, concat_axis=0, tiled=True),
    )
    wanted = jnp.arange(BAL)[:, None] == arrived_labels[None, :]
    placed = jnp.dot(
        wanted.astype(jnp.bfloat16), arrived, preferred_element_type=jnp.float32
    ).astype(jnp.bfloat16)
    return placed.reshape(BAL * CH, columns)


def per_device(
    queries,
    keys,
    values,
    out_weight,
    norm_gain,
    tile_counts,
    route_device,
    route_slot,
    session_starts,
):
    ctx_size = lax.axis_size("ctx")
    my_rank = lax.axis_index("ctx")
    slot_count = route_device.shape[0]
    row_count = slot_count * CH
    feature_width = queries.shape[1]
    head_count = feature_width // DH
    rank_ids = jnp.arange(ctx_size, dtype=jnp.int32)
    offset = CH * jnp.sum(jnp.where(rank_ids < my_rank, tile_counts, 0))
    my_count = jnp.sum(jnp.where(rank_ids == my_rank, tile_counts, 0))
    local_rows = jnp.arange(row_count, dtype=jnp.int32)
    is_live = local_rows // CH < my_count
    session = session_of(session_starts, offset + local_rows)
    prev_sess = session_of(session_starts, jnp.reshape(offset - 1, (1,)))[0]
    last_sess = session_of(session_starts, jnp.reshape(offset + my_count * CH - 1, (1,)))[0]
    query_feature_map = feature(queries).reshape(row_count, head_count, DH)
    key_map = feature(keys).reshape(row_count, head_count, DH)
    value_row_block = values.reshape(row_count, head_count, DH)
    key_mask = (is_live & (session == last_sess)).astype(jnp.bfloat16)
    masked_scores = key_map * key_mask[:, None, None]
    entry_value = jnp.einsum(
        "pld,plw->ldw", masked_scores, value_row_block, preferred_element_type=jnp.float32
    )
    reset_flag = (last_sess != prev_sess).astype(jnp.float32)
    carried = carried_in(
        (reset_flag, entry_value),
        "ctx",
        combine_states,
        (jnp.zeros((), jnp.float32), jnp.zeros_like(entry_value)),
    )
    incoming = carried[1]
    scores = jnp.einsum(
        "thd,shd->hts", query_feature_map, key_map, preferred_element_type=jnp.float32
    )
    allowed = (
        (local_rows[None, :] <= local_rows[:, None])
        & (session[None, :] == session[:, None])
        & is_live[None, :]
    )
    scores = jnp.where(allowed[None], scores, 0.0)
    score_upper, score_lower = split_parts(scores)
    inside = jnp.einsum(
        "hts,shd->thd", score_upper, value_row_block, preferred_element_type=jnp.float32
    )
    inside = inside + jnp.einsum(
        "hts,shd->thd", score_lower, value_row_block, preferred_element_type=jnp.float32
    )
    upper_state_half, lower_state_half = split_parts(incoming)
    carried_portion = jnp.einsum(
        "ycu,cux->ycx", query_feature_map, upper_state_half, preferred_element_type=jnp.float32
    )
    carried_portion = carried_portion + jnp.einsum(
        "ycu,cux->ycx", query_feature_map, lower_state_half, preferred_element_type=jnp.float32
    )
    carried_portion = jnp.where((session == prev_sess)[:, None, None], carried_portion, 0.0)
    numerator = inside + carried_portion
    inverse_rms = lax.rsqrt(jnp.mean(numerator * numerator, axis=-1, keepdims=True) + EPSILON)
    attended = (
        (numerator * inverse_rms * norm_gain.reshape(head_count, DH))
        .astype(jnp.bfloat16)
        .reshape(row_count, feature_width)
    )
    delivered = deliver(attended, route_device, route_slot, ctx_size)
    partial_value = jnp.dot(delivered, out_weight, preferred_element_type=jnp.float32)
    return lax.psum_scatter(
        partial_value.astype(jnp.bfloat16), "head", scatter_dimension=1, tiled=True
    )


def solution(mesh):
    placed = (
        P("ctx", "head"),
        P("ctx", "head"),
        P("ctx", "head"),
        P("head", None),
        P("head"),
        P(),
        P("ctx"),
        P("ctx"),
        P(),
    )
    return jax.shard_map(
        per_device, mesh=mesh, in_specs=placed, out_specs=P("ctx", "head"), check_vma=False
    )
```

```python
import functools

import jax
import jax.numpy as jnp
from jax import lax
from jax.experimental import pallas as pl
from jax.experimental.pallas import tpu as pltpu
from jax.sharding import PartitionSpec as P

DH = 128
CH = 8
BAL = 32


EPSILON = 1e-06


MESH = pl.DeviceIdType.MESH
STEP = 256


def offsets_far_first(n):
    order = sorted(range(1, n), key=lambda o: -min(o, n - o))
    return order


def greet(targets):
    barrier = pltpu.get_barrier_semaphore()
    for target in targets:
        pl.semaphore_signal(barrier, inc=1, device_id=target, device_id_type=MESH)
    pl.semaphore_wait(barrier, len(targets))


def state_kernel(
    n, heads, coef_ref, own_ref, sent_ref, labels_ref, inc_ref, got_ref,
    pair_in, chain_in, chain_out, pair_send, pair_recv, chain_send, chain_recv, lab_send, lab_recv, lab_own,
):
    me = lax.axis_index("ctx")
    pair, side = me // 2, me % 2
    partner = me + 1 - 2 * side
    has_prev = pair > 0
    has_next = pair < n // 2 - 1
    greet([{"ctx": lax.rem(me + o, n)} for o in range(1, n)])

    def pair_copy(h):
        return pltpu.make_async_remote_copy(
            src_ref=sent_ref.at[h], dst_ref=pair_in.at[h], send_sem=pair_send.at[h], recv_sem=pair_recv.at[h],
            device_id={"ctx": partner}, device_id_type=MESH,
        )

    def chain_copy(h):
        return pltpu.make_async_remote_copy(
            src_ref=chain_out.at[h], dst_ref=chain_in.at[h], send_sem=chain_send.at[h], recv_sem=chain_recv.at[h],
            device_id={"ctx": lax.rem(me + 2, n)}, device_id_type=MESH,
        )

    def label_copy(o):
        return pltpu.make_async_remote_copy(
            src_ref=labels_ref.at[lax.rem(me + o, n)], dst_ref=got_ref.at[o], send_sem=lab_send.at[o],
            recv_sem=lab_recv.at[o], device_id={"ctx": lax.rem(me + o, n)}, device_id_type=MESH,
        )

    for h in range(heads):
        pair_copy(h).start()

    @pl.when(jnp.logical_not(has_prev))
    def _():
        chain_in[...] = jnp.zeros_like(chain_in)

    for h in range(heads):
        pair_copy(h).wait_recv()
        other = pair_in[h].astype(jnp.float32)
        total = coef_ref[0] * own_ref[h] + coef_ref[1] * other

        @pl.when(has_prev)
        def _():
            chain_copy(h).wait_recv()

        carried = chain_in[h].astype(jnp.float32)

        @pl.when(has_next)
        def _():
            chain_out[h] = (total + coef_ref[2] * carried).astype(jnp.bfloat16)
            chain_copy(h).start()

        inc_ref[h] = coef_ref[3] * other + coef_ref[4] * carried

    local = pltpu.make_async_copy(labels_ref.at[me], got_ref.at[0], lab_own)
    local.start()
    for o in range(1, n):
        label_copy(o).start()
    local.wait()
    for o in range(1, n):
        label_copy(o).wait()
    for h in range(heads):
        pair_copy(h).wait_send()

        @pl.when(has_next)
        def _():
            chain_copy(h).wait_send()


def exchange_states(coef, entry, labels, n):
    heads = entry.shape[0]
    vmem = pl.BlockSpec(memory_space=pltpu.VMEM)
    dma = pltpu.SemaphoreType.DMA
    return pl.pallas_call(
        functools.partial(state_kernel, n, heads),
        out_shape=(
            jax.ShapeDtypeStruct(entry.shape, jnp.float32),
            jax.ShapeDtypeStruct(labels.shape, jnp.int32),
        ),
        in_specs=[pl.BlockSpec(memory_space=pltpu.SMEM), vmem, vmem, vmem],
        out_specs=(vmem, vmem),
        scratch_shapes=[pltpu.VMEM(entry.shape, jnp.bfloat16)] * 3
        + [dma((heads,))] * 4
        + [dma((n,))] * 2
        + [dma(())],
        compiler_params=pltpu.CompilerParams(collective_id=0, has_side_effects=True, vmem_limit_bytes=32 << 20),
        name="states",
    )(coef, entry, entry.astype(jnp.bfloat16), labels)


def project_kernel(
    n, groups, steps, buckets_ref, wanted_ref, weight_ref, out_ref,
    weight, arrived, placed, s1, r1, s2, r2, s3, r3, keep,
    w_sem, a_send, a_recv, a_own, x1s, x1r, x2s, x2r, x3s, x3r,
):
    me = lax.axis_index("ctx")
    mine = lax.axis_index("head")
    a, b = mine // 2, mine % 2
    sib = 2 * a + 1 - b
    far = 2 * (1 - a) + b
    far_sib = 2 * (1 - a) + 1 - b
    order = offsets_far_first(n)
    width = steps * STEP
    targets = (far_sib, far, sib, mine)

    def load(i):
        return pltpu.make_async_copy(
            weight_ref.at[:, pl.ds(pl.multiple_of(targets[i] * width, width), width)], weight.at[i], w_sem.at[i]
        )

    for i in range(4):
        load(i).start()
    greet([{"ctx": lax.rem(me + o, n)} for o in range(1, n)] + [{"head": sib}, {"head": far}])

    def tile_copy(o):
        to = lax.rem(me + o, n)
        return pltpu.make_async_remote_copy(
            src_ref=buckets_ref.at[to], dst_ref=arrived.at[o], send_sem=a_send.at[o], recv_sem=a_recv.at[o],
            device_id={"ctx": to}, device_id_type=MESH,
        )

    for o in order:
        tile_copy(o).start()
    local = pltpu.make_async_copy(buckets_ref.at[me], arrived.at[0], a_own)
    local.start()
    local.wait()
    for o in order:
        tile_copy(o).wait_recv()
    rows, depth = arrived.shape[0] * arrived.shape[1], arrived.shape[2]
    placed[...] = jnp.dot(
        wanted_ref[...], arrived[...].reshape(rows, depth), preferred_element_type=jnp.float32
    ).astype(jnp.bfloat16)

    def product(i, j):
        return jnp.dot(
            placed[...], weight[i, :, j * STEP : (j + 1) * STEP], preferred_element_type=jnp.float32
        )

    def move(src, dst, send, recv, j, to):
        return pltpu.make_async_remote_copy(
            src_ref=src.at[j], dst_ref=dst.at[j], send_sem=send.at[j], recv_sem=recv.at[j],
            device_id={"head": to}, device_id_type=MESH,
        )

    load(0).wait()
    for j in range(steps):
        s1[j] = product(0, j).astype(jnp.bfloat16)
        move(s1, r1, x1s, x1r, j, sib).start()
    load(1).wait()
    for j in range(steps):
        part = product(1, j)
        move(s1, r1, x1s, x1r, j, sib).wait_recv()
        s2[j] = (part.astype(jnp.bfloat16).astype(jnp.float32) + r1[j].astype(jnp.float32)).astype(jnp.bfloat16)
        move(s2, r2, x2s, x2r, j, far).start()
    load(2).wait()
    for j in range(steps):
        s3[j] = product(2, j).astype(jnp.bfloat16)
        move(s3, r3, x3s, x3r, j, sib).start()
    load(3).wait()
    for j in range(steps):
        keep[j] = product(3, j).astype(jnp.bfloat16).astype(jnp.float32)
    for j in range(steps):
        move(s3, r3, x3s, x3r, j, sib).wait_recv()
        near = keep[j] + r3[j].astype(jnp.float32)
        move(s2, r2, x2s, x2r, j, far).wait_recv()
        out_ref[:, j * STEP : (j + 1) * STEP] = (near + r2[j].astype(jnp.float32)).astype(jnp.bfloat16)
    for o in order:
        tile_copy(o).wait_send()
    for j in range(steps):
        move(s1, r1, x1s, x1r, j, sib).wait_send()
        move(s2, r2, x2s, x2r, j, far).wait_send()
        move(s3, r3, x3s, x3r, j, sib).wait_send()


def deliver_and_project(buckets, wanted, out_weight, n, groups):
    rows = wanted.shape[0]
    depth, columns = out_weight.shape
    width = columns // groups
    steps = width // STEP
    vmem = pl.BlockSpec(memory_space=pltpu.VMEM)
    dma = pltpu.SemaphoreType.DMA
    piece = pltpu.VMEM((steps, rows, STEP), jnp.bfloat16)
    return pl.pallas_call(
        functools.partial(project_kernel, n, groups, steps),
        out_shape=jax.ShapeDtypeStruct((rows, width), jnp.bfloat16),
        in_specs=[vmem, vmem, pl.BlockSpec(memory_space=pl.ANY)],
        out_specs=vmem,
        scratch_shapes=[
            pltpu.VMEM((groups, depth, width), jnp.bfloat16),
            pltpu.VMEM(buckets.shape, jnp.bfloat16),
            pltpu.VMEM((rows, depth), jnp.bfloat16),
            piece, piece, piece, piece, piece, piece,
            pltpu.VMEM((steps, rows, STEP), jnp.float32),
            dma((groups,)), dma((n,)), dma((n,)), dma(()),
        ]
        + [dma((steps,))] * 6,
        compiler_params=pltpu.CompilerParams(collective_id=1, has_side_effects=True, vmem_limit_bytes=40 << 20),
        name="deliver_project",
    )(buckets, wanted, out_weight)


def buckets_of(route_device, route_slot, ctx_size):
    slot_count = route_device.shape[0]
    capacity = (slot_count + ctx_size - 1) // ctx_size
    ordinal = jnp.arange(slot_count)
    clashes = (route_device[None, :] == route_device[:, None]) & (
        ordinal[None, :] < ordinal[:, None]
    )
    before = jnp.sum(clashes.astype(jnp.int32), axis=1)
    target = jnp.where(route_device >= 0, route_device * capacity + before, -1)
    chosen = jnp.arange(ctx_size * capacity)[:, None] == target[None, :]
    labels = jnp.sum(jnp.where(chosen, route_slot[None, :] + 1, 0), axis=1) - 1
    return chosen, labels, capacity


def feature(block):
    value = block.astype(jnp.float32)
    return jnp.where(value > 0, value + 1.0, jnp.exp(jnp.minimum(value, 0.0))).astype(jnp.bfloat16)


def split_parts(matrix):
    upper = matrix.astype(jnp.bfloat16)
    lower = (matrix - upper.astype(jnp.float32)).astype(jnp.bfloat16)
    return (upper, lower)


def session_of(session_starts, position):
    return jnp.sum((session_starts[None, :] <= position[:, None]).astype(jnp.int32), axis=1) - 1


def per_device(
    queries,
    keys,
    values,
    out_weight,
    norm_gain,
    tile_counts,
    route_device,
    route_slot,
    session_starts,
):
    ctx_size = lax.axis_size("ctx")
    my_rank = lax.axis_index("ctx")
    slot_count = route_device.shape[0]
    row_count = slot_count * CH
    feature_width = queries.shape[1]
    head_count = feature_width // DH
    rank_ids = jnp.arange(ctx_size, dtype=jnp.int32)
    offset = CH * jnp.sum(jnp.where(rank_ids < my_rank, tile_counts, 0))
    my_count = jnp.sum(jnp.where(rank_ids == my_rank, tile_counts, 0))
    local_rows = jnp.arange(row_count, dtype=jnp.int32)
    is_live = local_rows // CH < my_count
    session = session_of(session_starts, offset + local_rows)
    prev_sess = session_of(session_starts, jnp.reshape(offset - 1, (1,)))[0]
    last_sess = session_of(session_starts, jnp.reshape(offset + my_count * CH - 1, (1,)))[0]
    query_feature_map = feature(queries).reshape(row_count, head_count, DH)
    key_map = feature(keys).reshape(row_count, head_count, DH)
    value_row_block = values.reshape(row_count, head_count, DH)
    key_mask = (is_live & (session == last_sess)).astype(jnp.bfloat16)
    masked_scores = key_map * key_mask[:, None, None]
    entry_value = jnp.einsum(
        "pld,plw->ldw", masked_scores, value_row_block, preferred_element_type=jnp.float32
    )
    rank_last = session_of(session_starts, CH * jnp.cumsum(tile_counts) - 1)
    pair, side = my_rank // 2, my_rank % 2

    def last_of(index):
        return jnp.sum(jnp.where(rank_ids == index, rank_last, 0))

    before_pair = jnp.where(pair > 0, last_of(2 * pair - 1), -1)
    first, second = last_of(2 * pair), last_of(2 * pair + 1)
    joined = (first == second).astype(jnp.float32)
    one = jnp.float32(1.0)
    coef = jnp.stack(
        [
            jnp.where(side == 0, joined, one),
            jnp.where(side == 0, one, joined),
            (before_pair == second).astype(jnp.float32),
            side.astype(jnp.float32),
            jnp.where(side == 0, one, (before_pair == first).astype(jnp.float32)),
        ]
    )
    chosen, labels, capacity = buckets_of(route_device, route_slot, ctx_size)
    block = capacity * CH
    row_labels = labels.reshape(ctx_size, capacity)[:, :, None] * CH + jnp.arange(CH, dtype=jnp.int32)
    row_labels = jnp.where(labels.reshape(ctx_size, capacity, 1) >= 0, row_labels, -1).reshape(ctx_size, 1, block)
    label_block = jnp.broadcast_to(jnp.pad(row_labels, ((0, 0), (0, 0), (0, 128 - block))), (ctx_size, 8, 128))
    incoming, got = exchange_states(coef, entry_value, label_block, ctx_size)
    got_labels = got[:, 0, :block].reshape(ctx_size * block)
    wanted = (jnp.arange(BAL * CH, dtype=jnp.int32)[:, None] == got_labels[None, :]).astype(jnp.bfloat16)
    scores = jnp.einsum(
        "thd,shd->hts", query_feature_map, key_map, preferred_element_type=jnp.float32
    )
    allowed = (
        (local_rows[None, :] <= local_rows[:, None])
        & (session[None, :] == session[:, None])
        & is_live[None, :]
    )
    scores = jnp.where(allowed[None], scores, 0.0)
    score_upper, score_lower = split_parts(scores)
    inside = jnp.einsum(
        "hts,shd->thd", score_upper, value_row_block, preferred_element_type=jnp.float32
    )
    inside = inside + jnp.einsum(
        "hts,shd->thd", score_lower, value_row_block, preferred_element_type=jnp.float32
    )
    upper_state_half, lower_state_half = split_parts(incoming)
    carried_portion = jnp.einsum(
        "ycu,cux->ycx", query_feature_map, upper_state_half, preferred_element_type=jnp.float32
    )
    carried_portion = carried_portion + jnp.einsum(
        "ycu,cux->ycx", query_feature_map, lower_state_half, preferred_element_type=jnp.float32
    )
    carried_portion = jnp.where((session == prev_sess)[:, None, None], carried_portion, 0.0)
    numerator = inside + carried_portion
    inverse_rms = lax.rsqrt(jnp.mean(numerator * numerator, axis=-1, keepdims=True) + EPSILON)
    attended = (
        (numerator * inverse_rms * norm_gain.reshape(head_count, DH))
        .astype(jnp.bfloat16)
        .reshape(row_count, feature_width)
    )
    outgoing = jnp.dot(
        chosen.astype(jnp.bfloat16),
        attended.reshape(slot_count, CH * feature_width),
        preferred_element_type=jnp.float32,
    ).astype(jnp.bfloat16)
    return deliver_and_project(
        outgoing.reshape(ctx_size, block, feature_width), wanted, out_weight, ctx_size, lax.axis_size("head")
    )


def solution(mesh):
    placed = (
        P("ctx", "head"),
        P("ctx", "head"),
        P("ctx", "head"),
        P("head", None),
        P("head"),
        P(),
        P("ctx"),
        P("ctx"),
        P(),
    )
    return jax.shard_map(
        per_device, mesh=mesh, in_specs=placed, out_specs=P("ctx", "head"), check_vma=False
    )
```

```python
import functools

import jax
import jax.numpy as jnp
from jax import lax
from jax.experimental import pallas as pl
from jax.experimental.pallas import tpu as pltpu
from jax.sharding import PartitionSpec as P

DH = 128
CH = 8
BAL = 32


EPSILON = 1e-06


MESH = pl.DeviceIdType.MESH
STEP = 256


def offsets_far_first(n):
    order = sorted(range(1, n), key=lambda o: -min(o, n - o))
    return order


def greet(targets):
    barrier = pltpu.get_barrier_semaphore()
    for target in targets:
        pl.semaphore_signal(barrier, inc=1, device_id=target, device_id_type=MESH)
    pl.semaphore_wait(barrier, len(targets))


def feature(block):
    value = block.astype(jnp.float32)
    return jnp.where(value > 0, value + 1.0, jnp.exp(jnp.minimum(value, 0.0)))


def whole_kernel(
    n, groups, steps, parts, counts_ref, starts_ref, q_ref, k_ref, v_ref, gain_ref, target_ref, labels_ref, weight_ref, out_ref,
    kf, vf, mask, chosen, attended, own, sent, pair_in, chain_in, chain_out, got,
    buckets, arrived, total, weight, placed, s1, r1, s2, r2, s3, r3, keep,
    pair_send, pair_recv, chain_send, chain_recv, lab_send, lab_recv, lab_own,
    w_sem, a_send, a_recv, a_own, x1s, x1r, x2s, x2r, x3s, x3r,
):
    me = lax.axis_index("ctx")
    mine = lax.axis_index("head")
    a, b = mine // 2, mine % 2
    sib = 2 * a + 1 - b
    far = 2 * (1 - a) + b
    far_sib = 2 * (1 - a) + 1 - b
    pair, side = me // 2, me % 2
    partner = me + 1 - 2 * side
    has_prev = pair > 0
    has_next = pair < n // 2 - 1
    rows, features = q_ref.shape
    full = kf.shape[0]
    heads = features // DH
    span = features // parts
    order = offsets_far_first(n)
    width = steps * STEP
    targets = (far_sib, far, sib, mine)

    def load(i):
        return pltpu.make_async_copy(
            weight_ref.at[:, pl.ds(pl.multiple_of(targets[i] * width, width), width)], weight.at[i], w_sem.at[i]
        )

    def pair_copy(h):
        return pltpu.make_async_remote_copy(
            src_ref=sent.at[h], dst_ref=pair_in.at[h], send_sem=pair_send.at[h], recv_sem=pair_recv.at[h],
            device_id={"ctx": partner}, device_id_type=MESH,
        )

    def chain_copy(h):
        return pltpu.make_async_remote_copy(
            src_ref=chain_out.at[h], dst_ref=chain_in.at[h], send_sem=chain_send.at[h], recv_sem=chain_recv.at[h],
            device_id={"ctx": lax.rem(me + 2, n)}, device_id_type=MESH,
        )

    def label_copy(o):
        return pltpu.make_async_remote_copy(
            src_ref=labels_ref.at[lax.rem(me + o, n)], dst_ref=got.at[o], send_sem=lab_send.at[o],
            recv_sem=lab_recv.at[o], device_id={"ctx": lax.rem(me + o, n)}, device_id_type=MESH,
        )

    def tile_copy(g, o):
        to = lax.rem(me + o, n)
        return pltpu.make_async_remote_copy(
            src_ref=buckets.at[g, to], dst_ref=arrived.at[g, o], send_sem=a_send.at[g, o], recv_sem=a_recv.at[g, o],
            device_id={"ctx": to}, device_id_type=MESH,
        )

    def own_copy(g):
        return pltpu.make_async_copy(buckets.at[g, me], arrived.at[g, 0], a_own.at[g])

    def move(src, dst, send, recv, j, to):
        return pltpu.make_async_remote_copy(
            src_ref=src.at[j], dst_ref=dst.at[j], send_sem=send.at[j], recv_sem=recv.at[j],
            device_id={"head": to}, device_id_type=MESH,
        )

    for i in range(4):
        load(i).start()
    greet([{"ctx": lax.rem(me + o, n)} for o in range(1, n)] + [{"head": sib}, {"head": far}])

    counts = [counts_ref[i] for i in range(n)]

    def tiles_before(index):
        result = jnp.int32(0)
        for i in range(n):
            result = result + jnp.where(i < index, counts[i], 0)
        return result

    def session_at(position):
        result = jnp.zeros_like(position) - 1
        for i in range(starts_ref.shape[0]):
            result = result + jnp.where(starts_ref[i] <= position, 1, 0)
        return result

    def last_of(index):
        return session_at(CH * tiles_before(index + 1) - 1)

    def same(x, y):
        return jnp.where(x == y, jnp.float32(1.0), jnp.float32(0.0))

    offset = CH * tiles_before(me)
    live_end = CH * tiles_before(me + 1)
    last_sess, prev_sess = last_of(me), session_at(offset - 1)
    first, second = last_of(2 * pair), last_of(2 * pair + 1)
    before_pair = last_of(2 * pair - 1)
    joined = same(first, second)
    own_weight = jnp.where(side == 0, joined, 1.0)
    other_weight = jnp.where(side == 0, 1.0, joined)
    chain_weight = same(before_pair, second)
    inc_other = jnp.where(side == 0, 0.0, 1.0)
    inc_chain = jnp.where(side == 0, 1.0, same(before_pair, first))

    column = offset + lax.broadcasted_iota(jnp.int32, (full, DH), 0)
    column_sess = session_at(column)
    key_mask = jnp.where((column < live_end) & (column_sess == last_sess), 1.0, 0.0).astype(jnp.bfloat16)
    carry_mask = jnp.where(column_sess == prev_sess, 1.0, 0.0)

    def pad(block):
        return jnp.concatenate([block, jnp.zeros((full - rows, DH), jnp.float32)], axis=0)

    def columns_of(h):
        return pl.ds(pl.multiple_of(h * DH, DH), DH)

    def enter(h, _):
        cols = columns_of(h)
        key = pad(feature(k_ref[:, cols])).astype(jnp.bfloat16)
        value = pad(v_ref[:, cols].astype(jnp.float32)).astype(jnp.bfloat16)
        kf[:, cols] = key
        vf[:, cols] = value
        entry = lax.dot_general(
            key * key_mask, value, (((0,), (0,)), ((), ())), preferred_element_type=jnp.float32
        )
        own[h] = entry
        sent[h] = entry.astype(jnp.bfloat16)
        pair_copy(h).start()
        return 0

    lax.fori_loop(0, heads, enter, 0)

    for o in range(1, n):
        label_copy(o).start()
    label_own = pltpu.make_async_copy(labels_ref.at[me], got.at[0], lab_own)
    label_own.start()

    @pl.when(jnp.logical_not(has_prev))
    def _():
        chain_in[...] = jnp.zeros_like(chain_in)

    at_row = offset + lax.broadcasted_iota(jnp.int32, (full, full), 0)
    at_col = offset + lax.broadcasted_iota(jnp.int32, (full, full), 1)
    mask[...] = jnp.where(
        (at_col <= at_row) & (at_col < live_end) & (session_at(at_col) == session_at(at_row)), 1.0, 0.0
    ).astype(jnp.bfloat16)
    spots = buckets.shape[1] * buckets.shape[2]
    chosen[...] = jnp.where(
        lax.broadcasted_iota(jnp.int32, (spots, full), 0) == target_ref[...], 1.0, 0.0
    ).astype(jnp.bfloat16)
    half = full // 2

    def inner(h):
        cols = columns_of(h)
        query = pad(feature(q_ref[:, cols])).astype(jnp.bfloat16)

        def block(lo, hi):
            scores = lax.dot_general(
                query[lo:hi], kf[:hi, cols], (((1,), (1,)), ((), ())), preferred_element_type=jnp.float32
            )
            return jnp.dot(
                scores.astype(jnp.bfloat16) * mask[lo:hi, :hi], vf[:hi, cols], preferred_element_type=jnp.float32
            )

        return query, jnp.concatenate([block(0, half), block(half, full)], axis=0)

    def attend(h, _):
        cols = columns_of(h)
        query, inside = inner(h)
        pair_copy(h).wait_recv()
        other = pair_in[h].astype(jnp.float32)

        @pl.when(has_prev)
        def _():
            chain_copy(h).wait_recv()

        carried = chain_in[h].astype(jnp.float32)

        @pl.when(has_next)
        def _():
            chain_out[h] = (own_weight * own[h] + other_weight * other + chain_weight * carried).astype(jnp.bfloat16)
            chain_copy(h).start()

        incoming = (inc_other * other + inc_chain * carried).astype(jnp.bfloat16)
        numerator = inside + carry_mask * jnp.dot(query, incoming, preferred_element_type=jnp.float32)
        scale = lax.rsqrt(jnp.mean(numerator * numerator, axis=1, keepdims=True) + EPSILON)
        attended[:, cols] = (numerator * scale * gain_ref[:, cols]).astype(jnp.bfloat16)
        return 0

    for g in range(parts):
        lax.fori_loop(g * heads // parts, (g + 1) * heads // parts, attend, 0)
        buckets[g] = (
            jnp.dot(chosen[...], attended[:, g * span : (g + 1) * span], preferred_element_type=jnp.float32)
            .astype(jnp.bfloat16)
            .reshape(buckets.shape[1:])
        )
        for o in order:
            tile_copy(g, o).start()
        own_copy(g).start()

    label_own.wait()
    for o in range(1, n):
        label_copy(o).wait()

    here = lax.broadcasted_iota(jnp.int32, (total.shape[0], arrived.shape[2]), 0)
    for g in range(parts):
        own_copy(g).wait()
        for o in [0] + order[::-1]:
            if o:
                tile_copy(g, o).wait_recv()
            wanted = jnp.where(here == got[o, 0:1, : arrived.shape[2]], 1.0, 0.0).astype(jnp.bfloat16)
            term = jnp.dot(wanted, arrived[g, o], preferred_element_type=jnp.float32)
            if o:
                total[...] += term
            else:
                total[...] = term
        placed[:, g * span : (g + 1) * span] = total[...].astype(jnp.bfloat16)

    def product(i, j):
        return jnp.dot(
            placed[...], weight[i, :, j * STEP : (j + 1) * STEP], preferred_element_type=jnp.float32
        )

    load(0).wait()
    for j in range(steps):
        s1[j] = product(0, j).astype(jnp.bfloat16)
        move(s1, r1, x1s, x1r, j, sib).start()
    load(1).wait()
    for j in range(steps):
        part = product(1, j)
        move(s1, r1, x1s, x1r, j, sib).wait_recv()
        s2[j] = (part.astype(jnp.bfloat16).astype(jnp.float32) + r1[j].astype(jnp.float32)).astype(jnp.bfloat16)
        move(s2, r2, x2s, x2r, j, far).start()
    load(2).wait()
    for j in range(steps):
        s3[j] = product(2, j).astype(jnp.bfloat16)
        move(s3, r3, x3s, x3r, j, sib).start()
    load(3).wait()
    for j in range(steps):
        keep[j] = product(3, j).astype(jnp.bfloat16).astype(jnp.float32)
    for j in range(steps):
        move(s3, r3, x3s, x3r, j, sib).wait_recv()
        near = keep[j] + r3[j].astype(jnp.float32)
        move(s2, r2, x2s, x2r, j, far).wait_recv()
        out_ref[:, j * STEP : (j + 1) * STEP] = (near + r2[j].astype(jnp.float32)).astype(jnp.bfloat16)
    for g in range(parts):
        for o in order:
            tile_copy(g, o).wait_send()
    for h in range(heads):
        pair_copy(h).wait_send()

        @pl.when(has_next)
        def _():
            chain_copy(h).wait_send()

    for j in range(steps):
        move(s1, r1, x1s, x1r, j, sib).wait_send()
        move(s2, r2, x2s, x2r, j, far).wait_send()
        move(s3, r3, x3s, x3r, j, sib).wait_send()


def run_kernel(tile_counts, session_starts, queries, keys, values, gain, targets, labels, out_weight, n, groups, block):
    rows, depth = queries.shape
    full = n * block
    heads = depth // DH
    columns = out_weight.shape[1]
    width = columns // groups
    steps = width // STEP
    parts = 2
    out_rows = BAL * CH
    vmem = pl.BlockSpec(memory_space=pltpu.VMEM)
    smem = pl.BlockSpec(memory_space=pltpu.SMEM)
    dma = pltpu.SemaphoreType.DMA

    def half(*shape):
        return pltpu.VMEM(shape, jnp.bfloat16)

    def single(*shape):
        return pltpu.VMEM(shape, jnp.float32)

    return pl.pallas_call(
        functools.partial(whole_kernel, n, groups, steps, parts),
        out_shape=jax.ShapeDtypeStruct((out_rows, width), jnp.bfloat16),
        in_specs=[smem, smem, vmem, vmem, vmem, vmem, vmem, vmem, pl.BlockSpec(memory_space=pl.ANY)],
        out_specs=vmem,
        scratch_shapes=[half(full, depth)] * 2
        + [half(full, full)] * 2
        + [half(full, depth), single(heads, DH, DH)]
        + [half(heads, DH, DH)] * 4
        + [pltpu.VMEM(labels.shape, jnp.int32)]
        + [half(parts, n, block, depth // parts)] * 2
        + [single(out_rows, depth // parts), half(groups, depth, width), half(out_rows, depth)]
        + [half(steps, out_rows, STEP)] * 6
        + [single(steps, out_rows, STEP)]
        + [dma((heads,))] * 4
        + [dma((n,))] * 2
        + [dma(()), dma((groups,)), dma((parts, n)), dma((parts, n)), dma((parts,))]
        + [dma((steps,))] * 6,
        compiler_params=pltpu.CompilerParams(collective_id=0, has_side_effects=True, vmem_limit_bytes=56 << 20),
        name="layer",
    )(tile_counts, session_starts, queries, keys, values, gain, targets, labels, out_weight)


def per_device(
    queries, keys, values, out_weight, norm_gain, tile_counts, route_device, route_slot, session_starts
):
    ctx_size = lax.axis_size("ctx")
    slot_count = route_device.shape[0]
    capacity = (slot_count + ctx_size - 1) // ctx_size
    block = capacity * CH
    full = ctx_size * block
    ordinal = jnp.arange(slot_count)
    clashes = (route_device[None, :] == route_device[:, None]) & (ordinal[None, :] < ordinal[:, None])
    before = jnp.sum(clashes.astype(jnp.int32), axis=1)
    target = jnp.where(route_device >= 0, route_device * capacity + before, -1)
    chosen = jnp.arange(ctx_size * capacity)[:, None] == target[None, :]
    labels = jnp.sum(jnp.where(chosen, route_slot[None, :] + 1, 0), axis=1) - 1
    within = jnp.arange(CH, dtype=jnp.int32)
    row_targets = jnp.where(target >= 0, target * CH, -CH)[:, None] + within
    row_targets = jnp.pad(row_targets.reshape(1, slot_count * CH), ((0, 0), (0, full - slot_count * CH)), constant_values=-1)
    row_labels = jnp.where(labels >= 0, labels * CH, -CH)[:, None] + within
    row_labels = jnp.pad(row_labels.reshape(ctx_size, 1, block), ((0, 0), (0, 0), (0, 128 - block)), constant_values=-1)
    row_labels = jnp.broadcast_to(row_labels, (ctx_size, 8, 128))
    return run_kernel(
        tile_counts, session_starts, queries, keys, values, norm_gain.reshape(1, -1), row_targets, row_labels,
        out_weight, ctx_size, lax.axis_size("head"), block,
    )


def solution(mesh):
    placed = (
        P("ctx", "head"),
        P("ctx", "head"),
        P("ctx", "head"),
        P("head", None),
        P("head"),
        P(),
        P("ctx"),
        P("ctx"),
        P(),
    )
    return jax.shard_map(
        per_device, mesh=mesh, in_specs=placed, out_specs=P("ctx", "head"), check_vma=False
    )
```

```python
import functools

import jax
import jax.numpy as jnp
from jax import lax
from jax.experimental import pallas as pl
from jax.experimental.pallas import tpu as pltpu
from jax.sharding import PartitionSpec as P

DH = 128
CH = 8
BAL = 32


EPSILON = 1e-06


MESH = pl.DeviceIdType.MESH
STEP = 512
GROUPS = 4


def other_index(me, change):
    result, bit = 0, 1
    while bit <= change:
        if change & bit:
            result = result + bit * (1 - 2 * (lax.div(me, bit) % 2))
        bit *= 2
    return me + result


def feature(block):
    value = block.astype(jnp.float32)
    return jnp.where(value > 0, value + 1.0, jnp.exp(jnp.minimum(value, 0.0)))


def whole_kernel(
    n, groups, steps, parts, counts_ref, starts_ref, q_ref, k_ref, v_ref, gain_ref, route_ref, weight_ref, out_ref, got,
    kf, vf, mask, chosen, attended, own, sent, pair_in, chain_in, chain_out, labels_ref,
    buckets, arrived, weight, s1, r1, s2, r2, s3, r3, keep,
    pair_send, pair_recv, chain_send, chain_recv, lab_send, lab_recv, lab_own,
    w_sem, a_send, a_recv, a_own, x1s, x1r, x2s, x2r, x3s, x3r,
):
    me = lax.axis_index("ctx")
    mine = lax.axis_index("head")
    a, b = mine // 2, mine % 2
    sib = 2 * a + 1 - b
    far = 2 * (1 - a) + b
    far_sib = 2 * (1 - a) + 1 - b
    pair, side = me // 2, me % 2
    partner = me + 1 - 2 * side
    has_prev = pair > 0
    has_next = pair < n // 2 - 1
    rows, features = q_ref.shape
    full = kf.shape[0]
    heads = features // DH
    span = features // parts
    order = [n // 2 + o for o in range(n // 2)] + list(range(1, n // 2))
    block = buckets.shape[2]
    per_group = n // GROUPS
    width = steps * STEP
    targets = (far_sib, far, sib, mine)

    def load(i):
        return pltpu.make_async_copy(
            weight_ref.at[:, pl.ds(pl.multiple_of(targets[i] * width, width), width)], weight.at[i], w_sem.at[i]
        )

    def pair_copy(h):
        return pltpu.make_async_remote_copy(
            src_ref=sent.at[h], dst_ref=pair_in.at[h], send_sem=pair_send.at[h], recv_sem=pair_recv.at[h],
            device_id={"ctx": partner}, device_id_type=MESH,
        )

    def chain_copy(h):
        return pltpu.make_async_remote_copy(
            src_ref=chain_out.at[h], dst_ref=chain_in.at[h], send_sem=chain_send.at[h], recv_sem=chain_recv.at[h],
            device_id={"ctx": lax.rem(me + 2, n)}, device_id_type=MESH,
        )

    def label_copy(o):
        return pltpu.make_async_remote_copy(
            src_ref=labels_ref.at[other_index(me, o)], dst_ref=got.at[o], send_sem=lab_send.at[o],
            recv_sem=lab_recv.at[o], device_id={"ctx": other_index(me, o)}, device_id_type=MESH,
        )

    def tile_copy(g, o):
        to = other_index(me, o)
        return pltpu.make_async_remote_copy(
            src_ref=buckets.at[g, to], dst_ref=arrived.at[g, o], send_sem=a_send.at[g, o], recv_sem=a_recv.at[g, o],
            device_id={"ctx": to}, device_id_type=MESH,
        )

    def own_copy(g):
        return pltpu.make_async_copy(buckets.at[g, me], arrived.at[g, 0], a_own.at[g])

    def move(src, dst, send, recv, c, j, to):
        return pltpu.make_async_remote_copy(
            src_ref=src.at[c, j], dst_ref=dst.at[c, j], send_sem=send.at[c, j], recv_sem=recv.at[c, j],
            device_id={"head": to}, device_id_type=MESH,
        )

    for i in range(4):
        load(i).start()
    barrier = pltpu.get_barrier_semaphore()
    peers = [{"ctx": other_index(me, o)} for o in range(1, n)] + [{"head": sib}, {"head": far}]
    for peer in peers:
        pl.semaphore_signal(barrier, inc=1, device_id=peer, device_id_type=MESH)

    counts = [counts_ref[i] for i in range(n)]

    def tiles_before(index):
        result = jnp.int32(0)
        for i in range(n):
            result = result + jnp.where(i < index, counts[i], 0)
        return result

    def session_at(position):
        result = jnp.zeros_like(position) - 1
        for i in range(starts_ref.shape[0]):
            result = result + jnp.where(starts_ref[i] <= position, 1, 0)
        return result

    def last_of(index):
        return session_at(CH * tiles_before(index + 1) - 1)

    def same(x, y):
        return jnp.where(x == y, jnp.float32(1.0), jnp.float32(0.0))

    offset = CH * tiles_before(me)
    live_end = CH * tiles_before(me + 1)
    last_sess, prev_sess = last_of(me), session_at(offset - 1)
    first, second = last_of(2 * pair), last_of(2 * pair + 1)
    before_pair = last_of(2 * pair - 1)
    joined = same(first, second)
    own_weight = jnp.where(side == 0, joined, 1.0)
    other_weight = jnp.where(side == 0, 1.0, joined)
    chain_weight = same(before_pair, second)
    inc_other = jnp.where(side == 0, 0.0, 1.0)
    inc_chain = jnp.where(side == 0, 1.0, same(before_pair, first))

    column = offset + lax.broadcasted_iota(jnp.int32, (full, DH), 0)
    column_sess = session_at(column)
    key_mask = jnp.where((column < live_end) & (column_sess == last_sess), 1.0, 0.0).astype(jnp.bfloat16)
    carry_mask = jnp.where(column_sess == prev_sess, 1.0, 0.0)

    def pad(block):
        return jnp.concatenate([block, jnp.zeros((full - rows, DH), jnp.float32)], axis=0)

    def columns_of(h):
        return pl.ds(pl.multiple_of(h * DH, DH), DH)

    def enter(h, _):
        cols = columns_of(h)
        key = pad(feature(k_ref[:, cols])).astype(jnp.bfloat16)
        value = pad(v_ref[:, cols].astype(jnp.float32)).astype(jnp.bfloat16)
        kf[:, cols] = key
        vf[:, cols] = value
        entry = lax.dot_general(
            key * key_mask, value, (((0,), (0,)), ((), ())), preferred_element_type=jnp.float32
        )
        own[h] = entry
        sent[h] = entry.astype(jnp.bfloat16)
        return 0

    def enter_and_send(h, _):
        enter(h, 0)
        pair_copy(h).start()
        return 0

    early = 2
    lax.fori_loop(0, early, enter, 0)
    pl.semaphore_wait(barrier, len(peers))
    for h in range(early):
        pair_copy(h).start()
    lax.fori_loop(early, heads, enter_and_send, 0)

    lanes = route_ref.shape[1]
    capacity = block // CH
    device, slot = route_ref[0:1, :], route_ref[1:2, :]
    device_here = jnp.broadcast_to(device.astype(jnp.float32), (lanes, lanes))
    tile_row = lax.broadcasted_iota(jnp.int32, (lanes, lanes), 0)
    tile_col = lax.broadcasted_iota(jnp.int32, (lanes, lanes), 1)
    clash = (device_here == device_here.T) & (tile_row < tile_col)
    before = jnp.sum(jnp.where(clash, 1.0, 0.0), axis=0, keepdims=True).astype(jnp.int32)
    target = jnp.where(device >= 0, device * capacity + before, -1)
    token = lax.broadcasted_iota(jnp.int32, (lanes, full), 1)
    of_tile = jnp.where(token // CH == lax.broadcasted_iota(jnp.int32, (lanes, full), 0), 1.0, 0.0)
    target_tokens = jnp.dot(
        jnp.broadcast_to(target.astype(jnp.float32), (8, lanes)).astype(jnp.bfloat16),
        of_tile.astype(jnp.bfloat16),
        preferred_element_type=jnp.float32,
    )[0:1]
    target_rows = target_tokens.astype(jnp.int32) * CH + token[0:1] % CH
    tiles = n * capacity
    bucket = lax.broadcasted_iota(jnp.int32, (tiles, lanes), 0)
    lane = lax.broadcasted_iota(jnp.int32, (tiles, lanes), 1)
    label = jnp.sum(jnp.where(bucket == target, slot + 1, 0).astype(jnp.float32), axis=1, keepdims=True) - 1.0
    row_label = jnp.where(label >= 0.0, label * CH + (lane % CH).astype(jnp.float32), -1.0)
    row_label = jnp.where(lane // CH == bucket % capacity, row_label, 0.0)
    for d in range(n):
        one = jnp.sum(row_label[d * capacity : (d + 1) * capacity], axis=0, keepdims=True)
        labels_ref[d] = jnp.broadcast_to(one, (8, lanes)).astype(jnp.int32)

    for o in range(1, n):
        label_copy(o).start()
    label_own = pltpu.make_async_copy(labels_ref.at[me], got.at[0], lab_own)
    label_own.start()

    @pl.when(jnp.logical_not(has_prev))
    def _():
        chain_in[...] = jnp.zeros_like(chain_in)

    at_row = offset + lax.broadcasted_iota(jnp.int32, (full, full), 0)
    at_col = offset + lax.broadcasted_iota(jnp.int32, (full, full), 1)
    mask[...] = jnp.where(
        (at_col <= at_row) & (at_col < live_end) & (session_at(at_col) == session_at(at_row)), 1.0, 0.0
    ).astype(jnp.bfloat16)
    spots = buckets.shape[1] * buckets.shape[2]
    chosen[...] = jnp.where(
        lax.broadcasted_iota(jnp.int32, (spots, full), 0) == target_rows, 1.0, 0.0
    ).astype(jnp.bfloat16)
    half = full // 2

    def inner(h):
        cols = columns_of(h)
        query = pad(feature(q_ref[:, cols])).astype(jnp.bfloat16)

        def block(lo, hi):
            scores = lax.dot_general(
                query[lo:hi], kf[:hi, cols], (((1,), (1,)), ((), ())), preferred_element_type=jnp.float32
            )
            return jnp.dot(
                scores.astype(jnp.bfloat16) * mask[lo:hi, :hi], vf[:hi, cols], preferred_element_type=jnp.float32
            )

        return query, jnp.concatenate([block(0, half), block(half, full)], axis=0)

    def attend(h, _):
        cols = columns_of(h)
        query, inside = inner(h)
        pair_copy(h).wait_recv()
        other = pair_in[h].astype(jnp.float32)

        @pl.when(has_prev)
        def _():
            chain_copy(h).wait_recv()

        carried = chain_in[h].astype(jnp.float32)

        @pl.when(has_next)
        def _():
            chain_out[h] = (own_weight * own[h] + other_weight * other + chain_weight * carried).astype(jnp.bfloat16)
            chain_copy(h).start()

        incoming = (inc_other * other + inc_chain * carried).astype(jnp.bfloat16)
        numerator = inside + carry_mask * jnp.dot(query, incoming, preferred_element_type=jnp.float32)
        scale = lax.rsqrt(jnp.mean(numerator * numerator, axis=1, keepdims=True) + EPSILON)
        attended[:, cols] = (numerator * scale * gain_ref[:, cols]).astype(jnp.bfloat16)
        return 0

    for g in range(parts):
        lax.fori_loop(g * heads // parts, (g + 1) * heads // parts, attend, 0)
        buckets[g] = (
            jnp.dot(chosen[...], attended[:, g * span : (g + 1) * span], preferred_element_type=jnp.float32)
            .astype(jnp.bfloat16)
            .reshape(buckets.shape[1:])
        )
        for o in order:
            tile_copy(g, o).start()
        own_copy(g).start()

    label_own.wait()
    for o in range(1, n):
        label_copy(o).wait()

    def product(c, i, j):
        total = None
        for g in range(parts):
            rows_in = arrived[g, c * per_group : (c + 1) * per_group].reshape(per_group * block, span)
            term = jnp.dot(
                rows_in,
                weight[i, g * span : (g + 1) * span, j * STEP : (j + 1) * STEP],
                preferred_element_type=jnp.float32,
            )
            total = term if total is None else total + term
        return total.astype(jnp.bfloat16)

    def finish(c):
        for j in range(steps):
            move(s3, r3, x3s, x3r, c, j, sib).wait_recv()
            near = keep[c, j].astype(jnp.float32) + r3[c, j].astype(jnp.float32)
            move(s2, r2, x2s, x2r, c, j, far).wait_recv()
            out_ref[c * per_group * block : (c + 1) * per_group * block, j * STEP : (j + 1) * STEP] = (
                near + r2[c, j].astype(jnp.float32)
            ).astype(jnp.bfloat16)

    for c in range(GROUPS):
        for g in range(parts):
            for o in range(c * per_group, (c + 1) * per_group):
                if o:
                    tile_copy(g, o).wait_recv()
                else:
                    own_copy(g).wait()
        if c == 0:
            load(0).wait()
        for j in range(steps):
            s1[c, j] = product(c, 0, j)
            move(s1, r1, x1s, x1r, c, j, sib).start()
        if c == 0:
            load(1).wait()
        for j in range(steps):
            part = product(c, 1, j)
            move(s1, r1, x1s, x1r, c, j, sib).wait_recv()
            s2[c, j] = (part.astype(jnp.float32) + r1[c, j].astype(jnp.float32)).astype(jnp.bfloat16)
            move(s2, r2, x2s, x2r, c, j, far).start()
        if c == 0:
            load(2).wait()
        for j in range(steps):
            s3[c, j] = product(c, 2, j)
            move(s3, r3, x3s, x3r, c, j, sib).start()
        if c == 0:
            load(3).wait()
        for j in range(steps):
            keep[c, j] = product(c, 3, j)
        if c:
            finish(c - 1)
    finish(GROUPS - 1)
    for g in range(parts):
        for o in order:
            tile_copy(g, o).wait_send()
    for h in range(heads):
        pair_copy(h).wait_send()

        @pl.when(has_next)
        def _():
            chain_copy(h).wait_send()

    for c in range(GROUPS):
        for j in range(steps):
            move(s1, r1, x1s, x1r, c, j, sib).wait_send()
            move(s2, r2, x2s, x2r, c, j, far).wait_send()
            move(s3, r3, x3s, x3r, c, j, sib).wait_send()


def run_kernel(tile_counts, session_starts, queries, keys, values, gain, routes, out_weight, n, groups, block):
    rows, depth = queries.shape
    full = n * block
    heads = depth // DH
    columns = out_weight.shape[1]
    width = columns // groups
    steps = width // STEP
    parts = 2
    piece = (GROUPS, steps, full // GROUPS, STEP)
    got_shape = (n, 8, 128)
    vmem = pl.BlockSpec(memory_space=pltpu.VMEM)
    smem = pl.BlockSpec(memory_space=pltpu.SMEM)
    dma = pltpu.SemaphoreType.DMA

    def half(*shape):
        return pltpu.VMEM(shape, jnp.bfloat16)

    def single(*shape):
        return pltpu.VMEM(shape, jnp.float32)

    return pl.pallas_call(
        functools.partial(whole_kernel, n, groups, steps, parts),
        out_shape=(
            jax.ShapeDtypeStruct((full, width), jnp.bfloat16),
            jax.ShapeDtypeStruct(got_shape, jnp.int32),
        ),
        in_specs=[smem, smem, vmem, vmem, vmem, vmem, vmem, pl.BlockSpec(memory_space=pl.ANY)],
        out_specs=(vmem, vmem),
        scratch_shapes=[half(full, depth)] * 2
        + [half(full, full)] * 2
        + [half(full, depth), single(heads, DH, DH)]
        + [half(heads, DH, DH)] * 4
        + [pltpu.VMEM(got_shape, jnp.int32)]
        + [half(parts, n, block, depth // parts)] * 2
        + [half(groups, depth, width)]
        + [half(*piece)] * 7
        + [dma((heads,))] * 4
        + [dma((n,))] * 2
        + [dma(()), dma((groups,)), dma((parts, n)), dma((parts, n)), dma((parts,))]
        + [dma((GROUPS, steps))] * 6,
        compiler_params=pltpu.CompilerParams(collective_id=0, has_side_effects=True, vmem_limit_bytes=56 << 20),
        name="layer",
    )(tile_counts, session_starts, queries, keys, values, gain, routes, out_weight)


def per_device(
    queries, keys, values, out_weight, norm_gain, tile_counts, route_device, route_slot, session_starts
):
    ctx_size = lax.axis_size("ctx")
    slot_count = route_device.shape[0]
    capacity = (slot_count + ctx_size - 1) // ctx_size
    block = capacity * CH
    full = ctx_size * block
    routes = jnp.pad(jnp.stack([route_device, route_slot]), ((0, 0), (0, 128 - slot_count)), constant_values=-1)
    summed, got = run_kernel(
        tile_counts, session_starts, queries, keys, values, norm_gain.reshape(1, -1), routes, out_weight,
        ctx_size, lax.axis_size("head"), block,
    )
    labels = got[:, 0, :block].reshape(full)
    wanted = (jnp.arange(BAL * CH, dtype=jnp.int32)[:, None] == labels[None, :]).astype(jnp.bfloat16)
    return jnp.dot(wanted, summed, preferred_element_type=jnp.float32).astype(jnp.bfloat16)


def solution(mesh):
    placed = (
        P("ctx", "head"),
        P("ctx", "head"),
        P("ctx", "head"),
        P("head", None),
        P("head"),
        P(),
        P("ctx"),
        P("ctx"),
        P(),
    )
    return jax.shard_map(
        per_device, mesh=mesh, in_specs=placed, out_specs=P("ctx", "head"), check_vma=False
    )
```

```python
import functools

import jax
import jax.numpy as jnp
from jax import lax
from jax.experimental import pallas as pl
from jax.experimental.pallas import tpu as pltpu
from jax.sharding import PartitionSpec as P

DH = 128
CH = 8
BAL = 32


EPSILON = 1e-06


MESH = pl.DeviceIdType.MESH
STEP = 512
GROUPS = 4


def other_index(me, change):
    result, bit = 0, 1
    while bit <= change:
        if change & bit:
            result = result + bit * (1 - 2 * (lax.div(me, bit) % 2))
        bit *= 2
    return me + result


def feature(block):
    value = block.astype(jnp.float32)
    return jnp.where(value > 0, value + 1.0, jnp.exp(jnp.minimum(value, 0.0)))


def whole_kernel(
    n, groups, steps, parts, counts_ref, starts_ref, q_ref, k_ref, v_ref, gain_ref, route_ref, weight_ref, out_ref,
    got, placed, qf, inside, incoming, kf, vf, mask, chosen, attended, own, sent, pair_in, chain_in, chain_out, labels_ref,
    buckets, arrived, weight, s1, r1, s2, r2, s3, r3, keep,
    pair_send, pair_recv, chain_send, chain_recv, lab_send, lab_recv, lab_own,
    w_sem, a_send, a_recv, a_own, x1s, x1r, x2s, x2r, x3s, x3r,
):
    me = lax.axis_index("ctx")
    mine = lax.axis_index("head")
    a, b = mine // 2, mine % 2
    sib = 2 * a + 1 - b
    far = 2 * (1 - a) + b
    far_sib = 2 * (1 - a) + 1 - b
    pair, side = me // 2, me % 2
    partner = me + 1 - 2 * side
    has_prev = pair > 0
    has_next = pair < n // 2 - 1
    rows, features = q_ref.shape
    full = kf.shape[0]
    heads = features // DH
    span = features // parts
    order = [n // 2 + o for o in range(n // 2)] + list(range(1, n // 2))
    block = buckets.shape[2]
    per_group = n // GROUPS
    width = steps * STEP
    targets = (far_sib, far, sib, mine)

    def load(i):
        return pltpu.make_async_copy(
            weight_ref.at[:, pl.ds(pl.multiple_of(targets[i] * width, width), width)], weight.at[i], w_sem.at[i]
        )

    def pair_copy(h):
        return pltpu.make_async_remote_copy(
            src_ref=sent.at[h], dst_ref=pair_in.at[h], send_sem=pair_send.at[h], recv_sem=pair_recv.at[h],
            device_id={"ctx": partner}, device_id_type=MESH,
        )

    def chain_copy(h):
        return pltpu.make_async_remote_copy(
            src_ref=chain_out.at[h], dst_ref=chain_in.at[h], send_sem=chain_send.at[h], recv_sem=chain_recv.at[h],
            device_id={"ctx": lax.rem(me + 2, n)}, device_id_type=MESH,
        )

    def label_copy(o):
        return pltpu.make_async_remote_copy(
            src_ref=labels_ref.at[other_index(me, o)], dst_ref=got.at[o], send_sem=lab_send.at[o],
            recv_sem=lab_recv.at[o], device_id={"ctx": other_index(me, o)}, device_id_type=MESH,
        )

    def tile_copy(g, o):
        to = other_index(me, o)
        return pltpu.make_async_remote_copy(
            src_ref=buckets.at[g, to], dst_ref=arrived.at[g, o], send_sem=a_send.at[g, o], recv_sem=a_recv.at[g, o],
            device_id={"ctx": to}, device_id_type=MESH,
        )

    def own_copy(g):
        return pltpu.make_async_copy(buckets.at[g, me], arrived.at[g, 0], a_own.at[g])

    def move(src, dst, send, recv, c, j, to):
        return pltpu.make_async_remote_copy(
            src_ref=src.at[c, j], dst_ref=dst.at[c, j], send_sem=send.at[c, j], recv_sem=recv.at[c, j],
            device_id={"head": to}, device_id_type=MESH,
        )

    for i in range(4):
        load(i).start()
    barrier = pltpu.get_barrier_semaphore()
    peers = [{"ctx": other_index(me, o)} for o in range(1, n)] + [{"head": sib}, {"head": far}]
    for peer in peers:
        pl.semaphore_signal(barrier, inc=1, device_id=peer, device_id_type=MESH)

    counts = [counts_ref[i] for i in range(n)]

    def tiles_before(index):
        result = jnp.int32(0)
        for i in range(n):
            result = result + jnp.where(i < index, counts[i], 0)
        return result

    def session_at(position):
        result = jnp.zeros_like(position) - 1
        for i in range(starts_ref.shape[0]):
            result = result + jnp.where(starts_ref[i] <= position, 1, 0)
        return result

    def last_of(index):
        return session_at(CH * tiles_before(index + 1) - 1)

    def same(x, y):
        return jnp.where(x == y, jnp.float32(1.0), jnp.float32(0.0))

    offset = CH * tiles_before(me)
    live_end = CH * tiles_before(me + 1)
    last_sess, prev_sess = last_of(me), session_at(offset - 1)
    first, second = last_of(2 * pair), last_of(2 * pair + 1)
    before_pair = last_of(2 * pair - 1)
    joined = same(first, second)
    own_weight = jnp.where(side == 0, joined, 1.0)
    other_weight = jnp.where(side == 0, 1.0, joined)
    chain_weight = same(before_pair, second)
    inc_other = jnp.where(side == 0, 0.0, 1.0)
    inc_chain = jnp.where(side == 0, 1.0, same(before_pair, first))

    column = offset + lax.broadcasted_iota(jnp.int32, (full, DH), 0)
    column_sess = session_at(column)
    key_mask = jnp.where((column < live_end) & (column_sess == last_sess), 1.0, 0.0).astype(jnp.bfloat16)
    carry_mask = jnp.where(column_sess == prev_sess, 1.0, 0.0)

    def pad(block):
        return jnp.concatenate([block, jnp.zeros((full - rows, DH), jnp.float32)], axis=0)

    def columns_of(h):
        return pl.ds(pl.multiple_of(h * DH, DH), DH)

    def enter(h, _):
        cols = columns_of(h)
        key = pad(feature(k_ref[:, cols])).astype(jnp.bfloat16)
        value = pad(v_ref[:, cols].astype(jnp.float32)).astype(jnp.bfloat16)
        kf[:, cols] = key
        vf[:, cols] = value
        entry = lax.dot_general(
            key * key_mask, value, (((0,), (0,)), ((), ())), preferred_element_type=jnp.float32
        )
        own[h] = entry
        sent[h] = entry.astype(jnp.bfloat16)
        return 0

    def enter_and_send(p, _):
        for h in (2 * p, 2 * p + 1):
            enter(h, 0)
        for h in (2 * p, 2 * p + 1):
            pair_copy(h).start()
        return 0

    for h in range(2):
        enter(h, 0)
    pl.semaphore_wait(barrier, len(peers))
    for h in range(2):
        pair_copy(h).start()
    lax.fori_loop(1, heads // 2, enter_and_send, 0)

    lanes = route_ref.shape[1]
    capacity = block // CH
    device, slot = route_ref[0:1, :], route_ref[1:2, :]
    device_here = jnp.broadcast_to(device.astype(jnp.float32), (lanes, lanes))
    tile_row = lax.broadcasted_iota(jnp.int32, (lanes, lanes), 0)
    tile_col = lax.broadcasted_iota(jnp.int32, (lanes, lanes), 1)
    clash = (device_here == device_here.T) & (tile_row < tile_col)
    before = jnp.sum(jnp.where(clash, 1.0, 0.0), axis=0, keepdims=True).astype(jnp.int32)
    target = jnp.where(device >= 0, device * capacity + before, -1)
    token = lax.broadcasted_iota(jnp.int32, (lanes, full), 1)
    of_tile = jnp.where(token // CH == lax.broadcasted_iota(jnp.int32, (lanes, full), 0), 1.0, 0.0)
    target_tokens = jnp.dot(
        jnp.broadcast_to(target.astype(jnp.float32), (8, lanes)).astype(jnp.bfloat16),
        of_tile.astype(jnp.bfloat16),
        preferred_element_type=jnp.float32,
    )[0:1]
    target_rows = target_tokens.astype(jnp.int32) * CH + token[0:1] % CH
    tiles = n * capacity
    bucket = lax.broadcasted_iota(jnp.int32, (tiles, lanes), 0)
    lane = lax.broadcasted_iota(jnp.int32, (tiles, lanes), 1)
    label = jnp.sum(jnp.where(bucket == target, slot + 1, 0).astype(jnp.float32), axis=1, keepdims=True) - 1.0
    row_label = jnp.where(label >= 0.0, label * CH + (lane % CH).astype(jnp.float32), -1.0)
    row_label = jnp.where(lane // CH == bucket % capacity, row_label, 0.0)
    for d in range(n):
        one = jnp.sum(row_label[d * capacity : (d + 1) * capacity], axis=0, keepdims=True)
        labels_ref[d] = jnp.broadcast_to(one, (8, lanes)).astype(jnp.int32)

    for o in range(1, n):
        label_copy(o).start()
    label_own = pltpu.make_async_copy(labels_ref.at[me], got.at[0], lab_own)
    label_own.start()

    @pl.when(jnp.logical_not(has_prev))
    def _():
        chain_in[...] = jnp.zeros_like(chain_in)

    at_row = offset + lax.broadcasted_iota(jnp.int32, (full, full), 0)
    at_col = offset + lax.broadcasted_iota(jnp.int32, (full, full), 1)
    mask[...] = jnp.where(
        (at_col <= at_row) & (at_col < live_end) & (session_at(at_col) == session_at(at_row)), 1.0, 0.0
    ).astype(jnp.bfloat16)
    spots = buckets.shape[1] * buckets.shape[2]
    chosen[...] = jnp.where(
        lax.broadcasted_iota(jnp.int32, (spots, full), 0) == target_rows, 1.0, 0.0
    ).astype(jnp.bfloat16)
    half = full // 2

    def inner(h):
        cols = columns_of(h)
        query = pad(feature(q_ref[:, cols])).astype(jnp.bfloat16)

        def block(lo, hi):
            scores = lax.dot_general(
                query[lo:hi], kf[:hi, cols], (((1,), (1,)), ((), ())), preferred_element_type=jnp.float32
            )
            return jnp.dot(
                scores.astype(jnp.bfloat16) * mask[lo:hi, :hi], vf[:hi, cols], preferred_element_type=jnp.float32
            )

        qf[:, cols] = query
        inside[:half, cols] = block(0, half)
        inside[half:, cols] = block(half, full)

    def inner_two(p, _):
        inner(2 * p)
        inner(2 * p + 1)
        return 0

    def chain(h, _):
        pair_copy(h).wait_recv()
        other = pair_in[h].astype(jnp.float32)

        @pl.when(has_prev)
        def _():
            chain_copy(h).wait_recv()

        carried = chain_in[h].astype(jnp.float32)

        @pl.when(has_next)
        def _():
            chain_out[h] = (own_weight * own[h] + other_weight * other + chain_weight * carried).astype(jnp.bfloat16)
            chain_copy(h).start()

        incoming[h] = (inc_other * other + inc_chain * carried).astype(jnp.bfloat16)
        return 0

    def chain_and_inner(p, _):
        chain(2 * p, 0)
        chain(2 * p + 1, 0)
        return inner_two(p, 0)

    def attend(h):
        cols = columns_of(h)
        numerator = inside[:, cols] + carry_mask * jnp.dot(
            qf[:, cols], incoming[h], preferred_element_type=jnp.float32
        )
        scale = lax.rsqrt(jnp.mean(numerator * numerator, axis=1, keepdims=True) + EPSILON)
        attended[:, cols] = (numerator * scale * gain_ref[:, cols]).astype(jnp.bfloat16)

    def attend_two(p, _):
        attend(2 * p)
        attend(2 * p + 1)
        return 0

    lower = pair < n // 4

    @pl.when(lower)
    def _():
        lax.fori_loop(0, heads // 2, chain_and_inner, 0)

    @pl.when(jnp.logical_not(lower))
    def _():
        lax.fori_loop(0, heads // 2, inner_two, 0)
        lax.fori_loop(0, heads, chain, 0)

    for g in range(parts):
        lax.fori_loop(g * heads // parts // 2, (g + 1) * heads // parts // 2, attend_two, 0)
        buckets[g] = (
            jnp.dot(chosen[...], attended[:, g * span : (g + 1) * span], preferred_element_type=jnp.float32)
            .astype(jnp.bfloat16)
            .reshape(buckets.shape[1:])
        )
        for o in order:
            tile_copy(g, o).start()
        own_copy(g).start()

    label_own.wait()
    for o in range(1, n):
        label_copy(o).wait()

    def product(c, i, j):
        total = None
        for g in range(parts):
            rows_in = arrived[g, c * per_group : (c + 1) * per_group].reshape(per_group * block, span)
            term = jnp.dot(
                rows_in,
                weight[i, g * span : (g + 1) * span, j * STEP : (j + 1) * STEP],
                preferred_element_type=jnp.float32,
            )
            total = term if total is None else total + term
        return total.astype(jnp.bfloat16)

    def finish(c):
        names = jnp.concatenate(
            [got[o, 0:1, :block] for o in range(c * per_group, (c + 1) * per_group)], axis=1
        )
        here = lax.broadcasted_iota(jnp.int32, (out_ref.shape[0], per_group * block), 0)
        wanted = jnp.where(here == names, 1.0, 0.0).astype(jnp.bfloat16)
        for j in range(steps):
            move(s3, r3, x3s, x3r, c, j, sib).wait_recv()
            near = keep[c, j].astype(jnp.float32) + r3[c, j].astype(jnp.float32)
            move(s2, r2, x2s, x2r, c, j, far).wait_recv()
            summed = (near + r2[c, j].astype(jnp.float32)).astype(jnp.bfloat16)
            term = jnp.dot(wanted, summed, preferred_element_type=jnp.float32)
            if c == 0:
                placed[j] = term
            elif c < GROUPS - 1:
                placed[j] += term
            else:
                out_ref[:, j * STEP : (j + 1) * STEP] = (placed[j] + term).astype(jnp.bfloat16)

    for c in range(GROUPS):
        for g in range(parts):
            for o in range(c * per_group, (c + 1) * per_group):
                if o:
                    tile_copy(g, o).wait_recv()
                else:
                    own_copy(g).wait()
        if c == 0:
            load(0).wait()
        for j in range(steps):
            s1[c, j] = product(c, 0, j)
            move(s1, r1, x1s, x1r, c, j, sib).start()
        if c == 0:
            load(1).wait()
        for j in range(steps):
            part = product(c, 1, j)
            move(s1, r1, x1s, x1r, c, j, sib).wait_recv()
            s2[c, j] = (part.astype(jnp.float32) + r1[c, j].astype(jnp.float32)).astype(jnp.bfloat16)
            move(s2, r2, x2s, x2r, c, j, far).start()
        if c == 0:
            load(2).wait()
        for j in range(steps):
            s3[c, j] = product(c, 2, j)
            move(s3, r3, x3s, x3r, c, j, sib).start()
        if c == 0:
            load(3).wait()
        for j in range(steps):
            keep[c, j] = product(c, 3, j)
        if c:
            finish(c - 1)
    finish(GROUPS - 1)
    for g in range(parts):
        for o in order:
            tile_copy(g, o).wait_send()
    for h in range(heads):
        pair_copy(h).wait_send()

        @pl.when(has_next)
        def _():
            chain_copy(h).wait_send()

    for c in range(GROUPS):
        for j in range(steps):
            move(s1, r1, x1s, x1r, c, j, sib).wait_send()
            move(s2, r2, x2s, x2r, c, j, far).wait_send()
            move(s3, r3, x3s, x3r, c, j, sib).wait_send()


def run_kernel(tile_counts, session_starts, queries, keys, values, gain, routes, out_weight, n, groups, block):
    rows, depth = queries.shape
    full = n * block
    heads = depth // DH
    columns = out_weight.shape[1]
    width = columns // groups
    steps = width // STEP
    parts = 2
    piece = (GROUPS, steps, full // GROUPS, STEP)
    got_shape = (n, 8, 128)
    out_rows = BAL * CH
    vmem = pl.BlockSpec(memory_space=pltpu.VMEM)
    smem = pl.BlockSpec(memory_space=pltpu.SMEM)
    dma = pltpu.SemaphoreType.DMA

    def half(*shape):
        return pltpu.VMEM(shape, jnp.bfloat16)

    def single(*shape):
        return pltpu.VMEM(shape, jnp.float32)

    return pl.pallas_call(
        functools.partial(whole_kernel, n, groups, steps, parts),
        out_shape=jax.ShapeDtypeStruct((out_rows, width), jnp.bfloat16),
        in_specs=[smem, smem, vmem, vmem, vmem, vmem, vmem, pl.BlockSpec(memory_space=pl.ANY)],
        out_specs=vmem,
        scratch_shapes=[pltpu.VMEM(got_shape, jnp.int32), single(steps, out_rows, STEP)]
        + [half(full, depth), single(full, depth), half(heads, DH, DH)]
        + [half(full, depth)] * 2
        + [half(full, full)] * 2
        + [half(full, depth), single(heads, DH, DH)]
        + [half(heads, DH, DH)] * 4
        + [pltpu.VMEM(got_shape, jnp.int32)]
        + [half(parts, n, block, depth // parts)] * 2
        + [half(groups, depth, width)]
        + [half(*piece)] * 7
        + [dma((heads,))] * 4
        + [dma((n,))] * 2
        + [dma(()), dma((groups,)), dma((parts, n)), dma((parts, n)), dma((parts,))]
        + [dma((GROUPS, steps))] * 6,
        compiler_params=pltpu.CompilerParams(collective_id=0, has_side_effects=True, vmem_limit_bytes=56 << 20),
        name="layer",
    )(tile_counts, session_starts, queries, keys, values, gain, routes, out_weight)


def per_device(
    queries, keys, values, out_weight, norm_gain, tile_counts, route_device, route_slot, session_starts
):
    ctx_size = lax.axis_size("ctx")
    slot_count = route_device.shape[0]
    capacity = (slot_count + ctx_size - 1) // ctx_size
    block = capacity * CH
    full = ctx_size * block
    routes = jnp.pad(jnp.stack([route_device, route_slot]), ((0, 0), (0, 128 - slot_count)), constant_values=-1)
    return run_kernel(
        tile_counts, session_starts, queries, keys, values, norm_gain.reshape(1, -1), routes, out_weight,
        ctx_size, lax.axis_size("head"), block,
    )


def solution(mesh):
    placed = (
        P("ctx", "head"),
        P("ctx", "head"),
        P("ctx", "head"),
        P("head", None),
        P("head"),
        P(),
        P("ctx"),
        P("ctx"),
        P(),
    )
    return jax.shard_map(
        per_device, mesh=mesh, in_specs=placed, out_specs=P("ctx", "head"), check_vma=False
    )
```

```python
import functools

import jax
import jax.numpy as jnp
from jax import lax
from jax.experimental import pallas as pl
from jax.experimental.pallas import tpu as pltpu
from jax.sharding import PartitionSpec as P

DH = 128
CH = 8
BAL = 32


EPSILON = 1e-06


MESH = pl.DeviceIdType.MESH
STEP = 512
GROUPS = 4


def other_index(me, change):
    result, bit = 0, 1
    while bit <= change:
        if change & bit:
            result = result + bit * (1 - 2 * (lax.div(me, bit) % 2))
        bit *= 2
    return me + result


def feature(block):
    value = block.astype(jnp.float32)
    return jnp.where(value > 0, value + 1.0, jnp.exp(jnp.minimum(value, 0.0)))


def whole_kernel(
    n, groups, steps, parts, counts_ref, starts_ref, q_ref, k_ref, v_ref, gain_ref, route_ref, weight_ref, out_ref,
    got, placed, qf, inside, incoming, kf, vf, mask, chosen, attended, own, sent, pair_in, chain_in, chain_out, labels_ref,
    buckets, arrived, weight, s1, r1, s2, r2, s3, r3, keep,
    pair_send, pair_recv, chain_send, chain_recv, lab_send, lab_recv, lab_own,
    w_sem, a_send, a_recv, a_own, x1s, x1r, x2s, x2r, x3s, x3r,
):
    me = lax.axis_index("ctx")
    mine = lax.axis_index("head")
    a, b = mine // 2, mine % 2
    sib = 2 * a + 1 - b
    far = 2 * (1 - a) + b
    far_sib = 2 * (1 - a) + 1 - b
    pair, side = me // 2, me % 2
    partner = me + 1 - 2 * side
    has_prev = pair > 0
    has_next = pair < n // 2 - 1
    rows, features = q_ref.shape
    full = kf.shape[0]
    heads = features // DH
    span = features // parts
    order = [o for near in range(1, n // 2) for o in (near, n // 2 + near - 1)] + [n - 1]
    block = buckets.shape[2]
    per_group = n // GROUPS
    width = steps * STEP
    targets = (far_sib, far, sib, mine)

    def load(i):
        return pltpu.make_async_copy(
            weight_ref.at[:, pl.ds(pl.multiple_of(targets[i] * width, width), width)], weight.at[i], w_sem.at[i]
        )

    def pair_copy(h):
        return pltpu.make_async_remote_copy(
            src_ref=sent.at[h], dst_ref=pair_in.at[h], send_sem=pair_send.at[h], recv_sem=pair_recv.at[h],
            device_id={"ctx": partner}, device_id_type=MESH,
        )

    def chain_copy(h):
        return pltpu.make_async_remote_copy(
            src_ref=chain_out.at[h], dst_ref=chain_in.at[h], send_sem=chain_send.at[h], recv_sem=chain_recv.at[h],
            device_id={"ctx": lax.rem(me + 2, n)}, device_id_type=MESH,
        )

    def label_copy(o):
        return pltpu.make_async_remote_copy(
            src_ref=labels_ref.at[other_index(me, o)], dst_ref=got.at[o], send_sem=lab_send.at[o],
            recv_sem=lab_recv.at[o], device_id={"ctx": other_index(me, o)}, device_id_type=MESH,
        )

    def tile_copy(g, o):
        to = other_index(me, o)
        return pltpu.make_async_remote_copy(
            src_ref=buckets.at[g, to], dst_ref=arrived.at[g, o], send_sem=a_send.at[g, o], recv_sem=a_recv.at[g, o],
            device_id={"ctx": to}, device_id_type=MESH,
        )

    def own_copy(g):
        return pltpu.make_async_copy(buckets.at[g, me], arrived.at[g, 0], a_own.at[g])

    def move(src, dst, send, recv, c, j, to):
        return pltpu.make_async_remote_copy(
            src_ref=src.at[c, j], dst_ref=dst.at[c, j], send_sem=send.at[c, j], recv_sem=recv.at[c, j],
            device_id={"head": to}, device_id_type=MESH,
        )

    for i in range(4):
        load(i).start()
    barrier = pltpu.get_barrier_semaphore()
    peers = [{"ctx": other_index(me, o)} for o in range(1, n)] + [{"head": sib}, {"head": far}]
    for peer in peers:
        pl.semaphore_signal(barrier, inc=1, device_id=peer, device_id_type=MESH)

    counts = [counts_ref[i] for i in range(n)]

    def tiles_before(index):
        result = jnp.int32(0)
        for i in range(n):
            result = result + jnp.where(i < index, counts[i], 0)
        return result

    def session_at(position):
        result = jnp.zeros_like(position) - 1
        for i in range(starts_ref.shape[0]):
            result = result + jnp.where(starts_ref[i] <= position, 1, 0)
        return result

    def last_of(index):
        return session_at(CH * tiles_before(index + 1) - 1)

    def same(x, y):
        return jnp.where(x == y, jnp.float32(1.0), jnp.float32(0.0))

    offset = CH * tiles_before(me)
    live_end = CH * tiles_before(me + 1)
    last_sess, prev_sess = last_of(me), session_at(offset - 1)
    first, second = last_of(2 * pair), last_of(2 * pair + 1)
    before_pair = last_of(2 * pair - 1)
    joined = same(first, second)
    own_weight = jnp.where(side == 0, joined, 1.0)
    other_weight = jnp.where(side == 0, 1.0, joined)
    chain_weight = same(before_pair, second)
    inc_other = jnp.where(side == 0, 0.0, 1.0)
    inc_chain = jnp.where(side == 0, 1.0, same(before_pair, first))

    column = offset + lax.broadcasted_iota(jnp.int32, (full, DH), 0)
    column_sess = session_at(column)
    key_mask = jnp.where((column < live_end) & (column_sess == last_sess), 1.0, 0.0).astype(jnp.bfloat16)
    carry_mask = jnp.where(column_sess == prev_sess, 1.0, 0.0)

    def pad(block):
        return jnp.concatenate([block, jnp.zeros((full - rows, DH), jnp.float32)], axis=0)

    def columns_of(h):
        return pl.ds(pl.multiple_of(h * DH, DH), DH)

    def enter(h, _):
        cols = columns_of(h)
        key = pad(feature(k_ref[:, cols])).astype(jnp.bfloat16)
        value = pad(v_ref[:, cols].astype(jnp.float32)).astype(jnp.bfloat16)
        kf[:, cols] = key
        vf[:, cols] = value
        entry = lax.dot_general(
            key * key_mask, value, (((0,), (0,)), ((), ())), preferred_element_type=jnp.float32
        )
        own[h] = entry
        sent[h] = entry.astype(jnp.bfloat16)
        return 0

    def enter_and_send(p, _):
        for h in (2 * p, 2 * p + 1):
            enter(h, 0)
        for h in (2 * p, 2 * p + 1):
            pair_copy(h).start()
        return 0

    for h in range(2):
        enter(h, 0)
    pl.semaphore_wait(barrier, len(peers))
    for h in range(2):
        pair_copy(h).start()
    lax.fori_loop(1, heads // 2, enter_and_send, 0)

    lanes = route_ref.shape[1]
    capacity = block // CH
    device, slot = route_ref[0:1, :], route_ref[1:2, :]
    device_here = jnp.broadcast_to(device.astype(jnp.float32), (lanes, lanes))
    tile_row = lax.broadcasted_iota(jnp.int32, (lanes, lanes), 0)
    tile_col = lax.broadcasted_iota(jnp.int32, (lanes, lanes), 1)
    clash = (device_here == device_here.T) & (tile_row < tile_col)
    before = jnp.sum(jnp.where(clash, 1.0, 0.0), axis=0, keepdims=True).astype(jnp.int32)
    target = jnp.where(device >= 0, device * capacity + before, -1)
    token = lax.broadcasted_iota(jnp.int32, (lanes, full), 1)
    of_tile = jnp.where(token // CH == lax.broadcasted_iota(jnp.int32, (lanes, full), 0), 1.0, 0.0)
    target_tokens = jnp.dot(
        jnp.broadcast_to(target.astype(jnp.float32), (8, lanes)).astype(jnp.bfloat16),
        of_tile.astype(jnp.bfloat16),
        preferred_element_type=jnp.float32,
    )[0:1]
    target_rows = target_tokens.astype(jnp.int32) * CH + token[0:1] % CH
    tiles = n * capacity
    bucket = lax.broadcasted_iota(jnp.int32, (tiles, lanes), 0)
    lane = lax.broadcasted_iota(jnp.int32, (tiles, lanes), 1)
    label = jnp.sum(jnp.where(bucket == target, slot + 1, 0).astype(jnp.float32), axis=1, keepdims=True) - 1.0
    row_label = jnp.where(label >= 0.0, label * CH + (lane % CH).astype(jnp.float32), -1.0)
    row_label = jnp.where(lane // CH == bucket % capacity, row_label, 0.0)
    for d in range(n):
        one = jnp.sum(row_label[d * capacity : (d + 1) * capacity], axis=0, keepdims=True)
        labels_ref[d] = jnp.broadcast_to(one, (8, lanes)).astype(jnp.int32)

    for o in range(1, n):
        label_copy(o).start()
    label_own = pltpu.make_async_copy(labels_ref.at[me], got.at[0], lab_own)
    label_own.start()

    @pl.when(jnp.logical_not(has_prev))
    def _():
        chain_in[...] = jnp.zeros_like(chain_in)

    at_row = offset + lax.broadcasted_iota(jnp.int32, (full, full), 0)
    at_col = offset + lax.broadcasted_iota(jnp.int32, (full, full), 1)
    mask[...] = jnp.where(
        (at_col <= at_row) & (at_col < live_end) & (session_at(at_col) == session_at(at_row)), 1.0, 0.0
    ).astype(jnp.bfloat16)
    spots = buckets.shape[1] * buckets.shape[2]
    chosen[...] = jnp.where(
        lax.broadcasted_iota(jnp.int32, (spots, full), 0) == target_rows, 1.0, 0.0
    ).astype(jnp.bfloat16)
    half = full // 2

    def inner(h):
        cols = columns_of(h)
        query = pad(feature(q_ref[:, cols])).astype(jnp.bfloat16)

        def block(lo, hi):
            scores = lax.dot_general(
                query[lo:hi], kf[:hi, cols], (((1,), (1,)), ((), ())), preferred_element_type=jnp.float32
            )
            return jnp.dot(
                scores.astype(jnp.bfloat16) * mask[lo:hi, :hi], vf[:hi, cols], preferred_element_type=jnp.float32
            )

        qf[:, cols] = query
        inside[:half, cols] = block(0, half)
        inside[half:, cols] = block(half, full)

    def inner_two(p, _):
        inner(2 * p)
        inner(2 * p + 1)
        return 0

    def chain(h, _):
        pair_copy(h).wait_recv()
        other = pair_in[h].astype(jnp.float32)

        @pl.when(has_prev)
        def _():
            chain_copy(h).wait_recv()

        carried = chain_in[h].astype(jnp.float32)

        @pl.when(has_next)
        def _():
            chain_out[h] = (own_weight * own[h] + other_weight * other + chain_weight * carried).astype(jnp.bfloat16)
            chain_copy(h).start()

        incoming[h] = (inc_other * other + inc_chain * carried).astype(jnp.bfloat16)
        return 0

    def chain_and_inner(p, _):
        chain(2 * p, 0)
        chain(2 * p + 1, 0)
        return inner_two(p, 0)

    def attend(h):
        cols = columns_of(h)
        numerator = inside[:, cols] + carry_mask * jnp.dot(
            qf[:, cols], incoming[h], preferred_element_type=jnp.float32
        )
        scale = lax.rsqrt(jnp.mean(numerator * numerator, axis=1, keepdims=True) + EPSILON)
        attended[:, cols] = (numerator * scale * gain_ref[:, cols]).astype(jnp.bfloat16)

    def attend_two(p, _):
        attend(2 * p)
        attend(2 * p + 1)
        return 0

    lower = pair < n // 4

    @pl.when(lower)
    def _():
        lax.fori_loop(0, heads // 2, chain_and_inner, 0)

    @pl.when(jnp.logical_not(lower))
    def _():
        lax.fori_loop(0, heads // 2, inner_two, 0)
        lax.fori_loop(0, heads, chain, 0)

    for g in range(parts):
        lax.fori_loop(g * heads // parts // 2, (g + 1) * heads // parts // 2, attend_two, 0)
        buckets[g] = (
            jnp.dot(chosen[...], attended[:, g * span : (g + 1) * span], preferred_element_type=jnp.float32)
            .astype(jnp.bfloat16)
            .reshape(buckets.shape[1:])
        )
        for o in order:
            tile_copy(g, o).start()
        own_copy(g).start()

    label_own.wait()
    for o in range(1, n):
        label_copy(o).wait()

    def product(c, i, j):
        total = None
        for g in range(parts):
            rows_in = arrived[g, c * per_group : (c + 1) * per_group].reshape(per_group * block, span)
            term = jnp.dot(
                rows_in,
                weight[i, g * span : (g + 1) * span, j * STEP : (j + 1) * STEP],
                preferred_element_type=jnp.float32,
            )
            total = term if total is None else total + term
        return total.astype(jnp.bfloat16)

    def finish(c):
        names = jnp.concatenate(
            [got[o, 0:1, :block] for o in range(c * per_group, (c + 1) * per_group)], axis=1
        )
        here = lax.broadcasted_iota(jnp.int32, (out_ref.shape[0], per_group * block), 0)
        wanted = jnp.where(here == names, 1.0, 0.0).astype(jnp.bfloat16)
        for j in range(steps):
            move(s3, r3, x3s, x3r, c, j, sib).wait_recv()
            near = keep[c, j].astype(jnp.float32) + r3[c, j].astype(jnp.float32)
            move(s2, r2, x2s, x2r, c, j, far).wait_recv()
            summed = (near + r2[c, j].astype(jnp.float32)).astype(jnp.bfloat16)
            term = jnp.dot(wanted, summed, preferred_element_type=jnp.float32)
            if c == 0:
                placed[j] = term
            elif c < GROUPS - 1:
                placed[j] += term
            else:
                out_ref[:, j * STEP : (j + 1) * STEP] = (placed[j] + term).astype(jnp.bfloat16)

    for c in range(GROUPS):
        for g in range(parts):
            for o in range(c * per_group, (c + 1) * per_group):
                if o:
                    tile_copy(g, o).wait_recv()
                else:
                    own_copy(g).wait()
        if c == 0:
            load(0).wait()
        for j in range(steps):
            s1[c, j] = product(c, 0, j)
            move(s1, r1, x1s, x1r, c, j, sib).start()
        if c == 0:
            load(1).wait()
        for j in range(steps):
            part = product(c, 1, j)
            move(s1, r1, x1s, x1r, c, j, sib).wait_recv()
            s2[c, j] = (part.astype(jnp.float32) + r1[c, j].astype(jnp.float32)).astype(jnp.bfloat16)
            move(s2, r2, x2s, x2r, c, j, far).start()
        if c == 0:
            load(2).wait()
        for j in range(steps):
            s3[c, j] = product(c, 2, j)
            move(s3, r3, x3s, x3r, c, j, sib).start()
        if c == 0:
            load(3).wait()
        for j in range(steps):
            keep[c, j] = product(c, 3, j)
        if c:
            finish(c - 1)
    finish(GROUPS - 1)
    for g in range(parts):
        for o in order:
            tile_copy(g, o).wait_send()
    for h in range(heads):
        pair_copy(h).wait_send()

        @pl.when(has_next)
        def _():
            chain_copy(h).wait_send()

    for c in range(GROUPS):
        for j in range(steps):
            move(s1, r1, x1s, x1r, c, j, sib).wait_send()
            move(s2, r2, x2s, x2r, c, j, far).wait_send()
            move(s3, r3, x3s, x3r, c, j, sib).wait_send()


def run_kernel(tile_counts, session_starts, queries, keys, values, gain, routes, out_weight, n, groups, block):
    rows, depth = queries.shape
    full = n * block
    heads = depth // DH
    columns = out_weight.shape[1]
    width = columns // groups
    steps = width // STEP
    parts = 2
    piece = (GROUPS, steps, full // GROUPS, STEP)
    got_shape = (n, 8, 128)
    out_rows = BAL * CH
    vmem = pl.BlockSpec(memory_space=pltpu.VMEM)
    smem = pl.BlockSpec(memory_space=pltpu.SMEM)
    dma = pltpu.SemaphoreType.DMA

    def half(*shape):
        return pltpu.VMEM(shape, jnp.bfloat16)

    def single(*shape):
        return pltpu.VMEM(shape, jnp.float32)

    return pl.pallas_call(
        functools.partial(whole_kernel, n, groups, steps, parts),
        out_shape=jax.ShapeDtypeStruct((out_rows, width), jnp.bfloat16),
        in_specs=[smem, smem, vmem, vmem, vmem, vmem, vmem, pl.BlockSpec(memory_space=pl.ANY)],
        out_specs=vmem,
        scratch_shapes=[pltpu.VMEM(got_shape, jnp.int32), single(steps, out_rows, STEP)]
        + [half(full, depth), single(full, depth), half(heads, DH, DH)]
        + [half(full, depth)] * 2
        + [half(full, full)] * 2
        + [half(full, depth), single(heads, DH, DH)]
        + [half(heads, DH, DH)] * 4
        + [pltpu.VMEM(got_shape, jnp.int32)]
        + [half(parts, n, block, depth // parts)] * 2
        + [half(groups, depth, width)]
        + [half(*piece)] * 7
        + [dma((heads,))] * 4
        + [dma((n,))] * 2
        + [dma(()), dma((groups,)), dma((parts, n)), dma((parts, n)), dma((parts,))]
        + [dma((GROUPS, steps))] * 6,
        compiler_params=pltpu.CompilerParams(collective_id=0, has_side_effects=True, vmem_limit_bytes=56 << 20),
        name="layer",
    )(tile_counts, session_starts, queries, keys, values, gain, routes, out_weight)


def per_device(
    queries, keys, values, out_weight, norm_gain, tile_counts, route_device, route_slot, session_starts
):
    ctx_size = lax.axis_size("ctx")
    slot_count = route_device.shape[0]
    capacity = (slot_count + ctx_size - 1) // ctx_size
    block = capacity * CH
    full = ctx_size * block
    routes = jnp.pad(jnp.stack([route_device, route_slot]), ((0, 0), (0, 128 - slot_count)), constant_values=-1)
    return run_kernel(
        tile_counts, session_starts, queries, keys, values, norm_gain.reshape(1, -1), routes, out_weight,
        ctx_size, lax.axis_size("head"), block,
    )


def solution(mesh):
    placed = (
        P("ctx", "head"),
        P("ctx", "head"),
        P("ctx", "head"),
        P("head", None),
        P("head"),
        P(),
        P("ctx"),
        P("ctx"),
        P(),
    )
    return jax.shard_map(
        per_device, mesh=mesh, in_specs=placed, out_specs=P("ctx", "head"), check_vma=False
    )
```

```python
import functools

import jax
import jax.numpy as jnp
from jax import lax
from jax.experimental import pallas as pl
from jax.experimental.pallas import tpu as pltpu
from jax.sharding import PartitionSpec as P

DH = 128
CH = 8
BAL = 32


EPSILON = 1e-06


MESH = pl.DeviceIdType.MESH
STEP = 512
GROUPS = 4


def other_index(me, change):
    result, bit = 0, 1
    while bit <= change:
        if change & bit:
            result = result + bit * (1 - 2 * (lax.div(me, bit) % 2))
        bit *= 2
    return me + result


def feature(block):
    value = block.astype(jnp.float32)
    return jnp.where(value > 0, value + 1.0, jnp.exp(jnp.minimum(value, 0.0)))


def whole_kernel(
    n, groups, steps, parts, counts_ref, starts_ref, q_ref, k_ref, v_ref, gain_ref, route_ref, weight_ref, out_ref,
    got, placed, qf, inside, incoming, kf, vf, mask, chosen, attended, own, sent, pair_in, chain_in, chain_out, labels_ref,
    buckets, arrived, weight, s1, r1, s2, r2, s3, r3, keep,
    pair_send, pair_recv, chain_send, chain_recv, lab_send, lab_recv, lab_own,
    w_sem, a_send, a_recv, a_own, x1s, x1r, x2s, x2r, x3s, x3r,
):
    me = lax.axis_index("ctx")
    mine = lax.axis_index("head")
    a, b = mine // 2, mine % 2
    sib = 2 * a + 1 - b
    far = 2 * (1 - a) + b
    far_sib = 2 * (1 - a) + 1 - b
    pair, side = me // 2, me % 2
    partner = me + 1 - 2 * side
    has_prev = pair > 0
    has_next = pair < n // 2 - 1
    rows, features = q_ref.shape
    full = kf.shape[0]
    heads = features // DH
    span = features // parts
    order = [o for near in range(1, n // 2) for o in (near, n // 2 + near - 1)] + [n - 1]
    block = buckets.shape[2]
    per_group = n // GROUPS
    width = steps * STEP
    targets = (far_sib, far, sib, mine)

    def load(i):
        return pltpu.make_async_copy(
            weight_ref.at[:, pl.ds(pl.multiple_of(targets[i] * width, width), width)], weight.at[i], w_sem.at[i]
        )

    def pair_copy(h):
        return pltpu.make_async_remote_copy(
            src_ref=sent.at[h], dst_ref=pair_in.at[h], send_sem=pair_send.at[h], recv_sem=pair_recv.at[h],
            device_id={"ctx": partner}, device_id_type=MESH,
        )

    def chain_copy(h):
        return pltpu.make_async_remote_copy(
            src_ref=chain_out.at[h], dst_ref=chain_in.at[h], send_sem=chain_send.at[h], recv_sem=chain_recv.at[h],
            device_id={"ctx": lax.rem(me + 2, n)}, device_id_type=MESH,
        )

    def label_copy(o):
        return pltpu.make_async_remote_copy(
            src_ref=labels_ref.at[other_index(me, o)], dst_ref=got.at[o], send_sem=lab_send.at[o],
            recv_sem=lab_recv.at[o], device_id={"ctx": other_index(me, o)}, device_id_type=MESH,
        )

    def tile_copy(g, o):
        to = other_index(me, o)
        return pltpu.make_async_remote_copy(
            src_ref=buckets.at[g, to], dst_ref=arrived.at[g, o], send_sem=a_send.at[g, o], recv_sem=a_recv.at[g, o],
            device_id={"ctx": to}, device_id_type=MESH,
        )

    def own_copy(g):
        return pltpu.make_async_copy(buckets.at[g, me], arrived.at[g, 0], a_own.at[g])

    def move(src, dst, send, recv, c, j, to):
        return pltpu.make_async_remote_copy(
            src_ref=src.at[c, j], dst_ref=dst.at[c, j], send_sem=send.at[c, j], recv_sem=recv.at[c, j],
            device_id={"head": to}, device_id_type=MESH,
        )

    for i in range(4):
        load(i).start()
    barrier = pltpu.get_barrier_semaphore()
    peers = [{"ctx": other_index(me, o)} for o in range(1, n)] + [{"head": sib}, {"head": far}]
    for peer in peers:
        pl.semaphore_signal(barrier, inc=1, device_id=peer, device_id_type=MESH)

    counts = [counts_ref[i] for i in range(n)]

    def tiles_before(index):
        result = jnp.int32(0)
        for i in range(n):
            result = result + jnp.where(i < index, counts[i], 0)
        return result

    def session_at(position):
        result = jnp.zeros_like(position) - 1
        for i in range(starts_ref.shape[0]):
            result = result + jnp.where(starts_ref[i] <= position, 1, 0)
        return result

    def last_of(index):
        return session_at(CH * tiles_before(index + 1) - 1)

    def same(x, y):
        return jnp.where(x == y, jnp.float32(1.0), jnp.float32(0.0))

    offset = CH * tiles_before(me)
    live_end = CH * tiles_before(me + 1)
    last_sess, prev_sess = last_of(me), session_at(offset - 1)
    first, second = last_of(2 * pair), last_of(2 * pair + 1)
    before_pair = last_of(2 * pair - 1)
    joined = same(first, second)
    own_weight = jnp.where(side == 0, joined, 1.0)
    other_weight = jnp.where(side == 0, 1.0, joined)
    chain_weight = same(before_pair, second)
    inc_other = jnp.where(side == 0, 0.0, 1.0)
    inc_chain = jnp.where(side == 0, 1.0, same(before_pair, first))

    column = offset + lax.broadcasted_iota(jnp.int32, (full, DH), 0)
    column_sess = session_at(column)
    key_mask = jnp.where((column < live_end) & (column_sess == last_sess), 1.0, 0.0).astype(jnp.bfloat16)
    carry_mask = jnp.where(column_sess == prev_sess, 1.0, 0.0)

    def pad(block):
        return jnp.concatenate([block, jnp.zeros((full - rows, DH), jnp.float32)], axis=0)

    def columns_of(h):
        return pl.ds(pl.multiple_of(h * DH, DH), DH)

    def enter(h, _):
        cols = columns_of(h)
        key = pad(feature(k_ref[:, cols])).astype(jnp.bfloat16)
        value = pad(v_ref[:, cols].astype(jnp.float32)).astype(jnp.bfloat16)
        kf[:, cols] = key
        vf[:, cols] = value
        entry = lax.dot_general(
            key * key_mask, value, (((0,), (0,)), ((), ())), preferred_element_type=jnp.float32
        )
        own[h] = entry
        sent[h] = entry.astype(jnp.bfloat16)
        return 0

    def enter_and_send(p, _):
        for h in (2 * p, 2 * p + 1):
            enter(h, 0)
        for h in (2 * p, 2 * p + 1):
            pair_copy(h).start()
        return 0

    for h in range(2):
        enter(h, 0)
    pl.semaphore_wait(barrier, len(peers))
    for h in range(2):
        pair_copy(h).start()
    lax.fori_loop(1, heads // 2, enter_and_send, 0)

    lanes = route_ref.shape[1]
    capacity = block // CH
    device, slot = route_ref[0:1, :], route_ref[1:2, :]
    device_here = jnp.broadcast_to(device.astype(jnp.float32), (lanes, lanes))
    tile_row = lax.broadcasted_iota(jnp.int32, (lanes, lanes), 0)
    tile_col = lax.broadcasted_iota(jnp.int32, (lanes, lanes), 1)
    clash = (device_here == device_here.T) & (tile_row < tile_col)
    before = jnp.sum(jnp.where(clash, 1.0, 0.0), axis=0, keepdims=True).astype(jnp.int32)
    target = jnp.where(device >= 0, device * capacity + before, -1)
    token = lax.broadcasted_iota(jnp.int32, (lanes, full), 1)
    of_tile = jnp.where(token // CH == lax.broadcasted_iota(jnp.int32, (lanes, full), 0), 1.0, 0.0)
    target_tokens = jnp.dot(
        jnp.broadcast_to(target.astype(jnp.float32), (8, lanes)).astype(jnp.bfloat16),
        of_tile.astype(jnp.bfloat16),
        preferred_element_type=jnp.float32,
    )[0:1]
    target_rows = target_tokens.astype(jnp.int32) * CH + token[0:1] % CH
    tiles = n * capacity
    bucket = lax.broadcasted_iota(jnp.int32, (tiles, lanes), 0)
    lane = lax.broadcasted_iota(jnp.int32, (tiles, lanes), 1)
    label = jnp.sum(jnp.where(bucket == target, slot + 1, 0).astype(jnp.float32), axis=1, keepdims=True) - 1.0
    row_label = jnp.where(label >= 0.0, label * CH + (lane % CH).astype(jnp.float32), -1.0)
    row_label = jnp.where(lane // CH == bucket % capacity, row_label, 0.0)
    for d in range(n):
        one = jnp.sum(row_label[d * capacity : (d + 1) * capacity], axis=0, keepdims=True)
        labels_ref[d] = jnp.broadcast_to(one, (8, lanes)).astype(jnp.int32)

    for o in range(1, n):
        label_copy(o).start()
    label_own = pltpu.make_async_copy(labels_ref.at[me], got.at[0], lab_own)
    label_own.start()

    @pl.when(jnp.logical_not(has_prev))
    def _():
        chain_in[...] = jnp.zeros_like(chain_in)

    at_row = offset + lax.broadcasted_iota(jnp.int32, (full, full), 0)
    at_col = offset + lax.broadcasted_iota(jnp.int32, (full, full), 1)
    mask[...] = jnp.where(
        (at_col <= at_row) & (at_col < live_end) & (session_at(at_col) == session_at(at_row)), 1.0, 0.0
    ).astype(jnp.bfloat16)
    spots = buckets.shape[1] * buckets.shape[2]
    chosen[...] = jnp.where(
        lax.broadcasted_iota(jnp.int32, (spots, full), 0) == target_rows, 1.0, 0.0
    ).astype(jnp.bfloat16)
    half = full // 2

    def inner(h):
        cols = columns_of(h)
        query = pad(feature(q_ref[:, cols])).astype(jnp.bfloat16)

        def block(lo, hi):
            scores = lax.dot_general(
                query[lo:hi], kf[:hi, cols], (((1,), (1,)), ((), ())), preferred_element_type=jnp.float32
            )
            return jnp.dot(
                scores.astype(jnp.bfloat16) * mask[lo:hi, :hi], vf[:hi, cols], preferred_element_type=jnp.float32
            )

        qf[:, cols] = query
        inside[:half, cols] = block(0, half)
        inside[half:, cols] = block(half, full)

    def inner_two(p, _):
        inner(2 * p)
        inner(2 * p + 1)
        return 0

    def chain(h, _):
        pair_copy(h).wait_recv()
        other = pair_in[h].astype(jnp.float32)

        @pl.when(has_prev)
        def _():
            chain_copy(h).wait_recv()

        carried = chain_in[h].astype(jnp.float32)

        @pl.when(has_next)
        def _():
            chain_out[h] = (own_weight * own[h] + other_weight * other + chain_weight * carried).astype(jnp.bfloat16)
            chain_copy(h).start()

        incoming[h] = (inc_other * other + inc_chain * carried).astype(jnp.bfloat16)
        return 0

    def chain_and_inner(p, _):
        chain(2 * p, 0)
        chain(2 * p + 1, 0)
        return inner_two(p, 0)

    def attend(h):
        cols = columns_of(h)
        numerator = inside[:, cols] + carry_mask * jnp.dot(
            qf[:, cols], incoming[h], preferred_element_type=jnp.float32
        )
        scale = lax.rsqrt(jnp.mean(numerator * numerator, axis=1, keepdims=True) + EPSILON)
        attended[:, cols] = (numerator * scale * gain_ref[:, cols]).astype(jnp.bfloat16)

    def attend_two(p, _):
        attend(2 * p)
        attend(2 * p + 1)
        return 0

    lower = pair < n // 4

    @pl.when(lower)
    def _():
        lax.fori_loop(0, heads // 2, chain_and_inner, 0)

    @pl.when(jnp.logical_not(lower))
    def _():
        lax.fori_loop(0, heads // 2, inner_two, 0)
        lax.fori_loop(0, heads, chain, 0)

    for g in range(parts):
        lax.fori_loop(g * heads // parts // 2, (g + 1) * heads // parts // 2, attend_two, 0)
        buckets[g] = (
            jnp.dot(chosen[...], attended[:, g * span : (g + 1) * span], preferred_element_type=jnp.float32)
            .astype(jnp.bfloat16)
            .reshape(buckets.shape[1:])
        )
        for o in order:
            tile_copy(g, o).start()
        own_copy(g).start()

    label_own.wait()
    for o in range(1, n):
        label_copy(o).wait()

    def product(c, i, j):
        total = None
        for g in range(parts):
            rows_in = arrived[g, c * per_group : (c + 1) * per_group].reshape(per_group * block, span)
            term = jnp.dot(
                rows_in,
                weight[i, g * span : (g + 1) * span, j * STEP : (j + 1) * STEP],
                preferred_element_type=jnp.float32,
            )
            total = term if total is None else total + term
        return total.astype(jnp.bfloat16)

    def finish(c):
        names = jnp.concatenate(
            [got[o, 0:1, :block] for o in range(c * per_group, (c + 1) * per_group)], axis=1
        )
        here = lax.broadcasted_iota(jnp.int32, (out_ref.shape[0], per_group * block), 0)
        wanted = jnp.where(here == names, 1.0, 0.0).astype(jnp.bfloat16)
        for j in range(steps):
            move(s3, r3, x3s, x3r, c, j, sib).wait_recv()
            near = keep[c, j].astype(jnp.float32) + r3[c, j].astype(jnp.float32)
            move(s2, r2, x2s, x2r, c, j, far).wait_recv()
            summed = (near + r2[c, j].astype(jnp.float32)).astype(jnp.bfloat16)
            term = jnp.dot(wanted, summed, preferred_element_type=jnp.float32)
            if c == 0:
                placed[j] = term
            elif c < GROUPS - 1:
                placed[j] += term
            else:
                out_ref[:, j * STEP : (j + 1) * STEP] = (placed[j] + term).astype(jnp.bfloat16)

    for c in range(GROUPS):
        for g in range(parts):
            for o in range(c * per_group, (c + 1) * per_group):
                if o:
                    tile_copy(g, o).wait_recv()
                else:
                    own_copy(g).wait()
        if c == 0:
            load(0).wait()
        for j in range(steps):
            s1[c, j] = product(c, 0, j)
            move(s1, r1, x1s, x1r, c, j, sib).start()
        if c == 0:
            load(1).wait()
        for j in range(steps):
            part = product(c, 1, j)
            move(s1, r1, x1s, x1r, c, j, sib).wait_recv()
            s2[c, j] = (part.astype(jnp.float32) + r1[c, j].astype(jnp.float32)).astype(jnp.bfloat16)
            move(s2, r2, x2s, x2r, c, j, far).start()
        if c == 0:
            load(2).wait()
        for j in range(steps):
            s3[c, j] = product(c, 2, j)
            move(s3, r3, x3s, x3r, c, j, sib).start()
        if c == 0:
            load(3).wait()
        for j in range(steps):
            keep[c, j] = product(c, 3, j)
        if c:
            finish(c - 1)
    finish(GROUPS - 1)
    for g in range(parts):
        for o in order:
            tile_copy(g, o).wait_send()
    for h in range(heads):
        pair_copy(h).wait_send()

        @pl.when(has_next)
        def _():
            chain_copy(h).wait_send()

    for c in range(GROUPS):
        for j in range(steps):
            move(s1, r1, x1s, x1r, c, j, sib).wait_send()
            move(s2, r2, x2s, x2r, c, j, far).wait_send()
            move(s3, r3, x3s, x3r, c, j, sib).wait_send()


def run_kernel(tile_counts, session_starts, queries, keys, values, gain, routes, out_weight, n, groups, block):
    rows, depth = queries.shape
    full = n * block
    heads = depth // DH
    columns = out_weight.shape[1]
    width = columns // groups
    steps = width // STEP
    parts = 1
    piece = (GROUPS, steps, full // GROUPS, STEP)
    got_shape = (n, 8, 128)
    out_rows = BAL * CH
    vmem = pl.BlockSpec(memory_space=pltpu.VMEM)
    smem = pl.BlockSpec(memory_space=pltpu.SMEM)
    dma = pltpu.SemaphoreType.DMA

    def half(*shape):
        return pltpu.VMEM(shape, jnp.bfloat16)

    def single(*shape):
        return pltpu.VMEM(shape, jnp.float32)

    return pl.pallas_call(
        functools.partial(whole_kernel, n, groups, steps, parts),
        out_shape=jax.ShapeDtypeStruct((out_rows, width), jnp.bfloat16),
        in_specs=[smem, smem, vmem, vmem, vmem, vmem, vmem, pl.BlockSpec(memory_space=pl.ANY)],
        out_specs=vmem,
        scratch_shapes=[pltpu.VMEM(got_shape, jnp.int32), single(steps, out_rows, STEP)]
        + [half(full, depth), single(full, depth), half(heads, DH, DH)]
        + [half(full, depth)] * 2
        + [half(full, full)] * 2
        + [half(full, depth), single(heads, DH, DH)]
        + [half(heads, DH, DH)] * 4
        + [pltpu.VMEM(got_shape, jnp.int32)]
        + [half(parts, n, block, depth // parts)] * 2
        + [half(groups, depth, width)]
        + [half(*piece)] * 7
        + [dma((heads,))] * 4
        + [dma((n,))] * 2
        + [dma(()), dma((groups,)), dma((parts, n)), dma((parts, n)), dma((parts,))]
        + [dma((GROUPS, steps))] * 6,
        compiler_params=pltpu.CompilerParams(collective_id=0, has_side_effects=True, vmem_limit_bytes=56 << 20),
        name="layer",
    )(tile_counts, session_starts, queries, keys, values, gain, routes, out_weight)


def per_device(
    queries, keys, values, out_weight, norm_gain, tile_counts, route_device, route_slot, session_starts
):
    ctx_size = lax.axis_size("ctx")
    slot_count = route_device.shape[0]
    capacity = (slot_count + ctx_size - 1) // ctx_size
    block = capacity * CH
    full = ctx_size * block
    routes = jnp.pad(jnp.stack([route_device, route_slot]), ((0, 0), (0, 128 - slot_count)), constant_values=-1)
    return run_kernel(
        tile_counts, session_starts, queries, keys, values, norm_gain.reshape(1, -1), routes, out_weight,
        ctx_size, lax.axis_size("head"), block,
    )


def solution(mesh):
    placed = (
        P("ctx", "head"),
        P("ctx", "head"),
        P("ctx", "head"),
        P("head", None),
        P("head"),
        P(),
        P("ctx"),
        P("ctx"),
        P(),
    )
    return jax.shard_map(
        per_device, mesh=mesh, in_specs=placed, out_specs=P("ctx", "head"), check_vma=False
    )
```
